512 devices in a mesh: date: 32 (over z, x), band: 16 (over y, core).
Axes of the slice: x: 4, y: 8, z: 8, core: 2. Of those that a mesh axis runs over, the one named last changes fastest.
Arguments:
- radar_image_cube: bfloat16 [32, 2, 320, 20480], P('date', None, 'band'), may hold values from -90 to 90
- orbit_separations: bfloat16 [32], P('date'), may hold values from -2 to 2
- epoch_couple_matrix: int32 [64, 2], P('date'), may hold values from 0 to 31, as said below
- averaged_line_grid_lines: int32 [64], P('band'), may hold values from 0 to 63, as said below
Outputs:
- ifg_map: float32 [64, 2, 64, 1024], P('date', None, 'band')
- coh_map: float32 [64, 64, 1024], P('date', 'band')
The draws below stay inside these ranges and needn't reach their ends.
Inputs may be any that keep to these rules, and one draw needn't show every extreme that they name: epoch_couple_matrix[p, 0] = p // 2; epoch_couple_matrix[p, 1] lies 1 to 3 dates from epoch_couple_matrix[p, 0], after it where that date exists, else before it; the two pairs of one date differ. averaged_line_grid_lines[r] differs from r by at most 4, and by exactly that much for some rows.
All inputs are finite; a program needn't handle non-finite values.
Results may differ from the reference program's by a relative error of at most 0.0003.
Values may be sent and summed in bfloat16 or wider, within the bound.
No kernel may reach another device: no remote copies, remote signals or barrier semaphores. Data moves between devices by JAX's collectives and lax.ppermute only.
A program may use at most 64 MiB of HBM per device.

```python
import math
import jax
import jax.numpy as jnp
from jax import lax

ROWS_DEV = 20
LOOK_R = 5
LOOK_C = 20
EPOCH_TOTAL = 32
PAIRS = 64
ROWS = 320
COLS = 20480
LOOK_ROWS = 64


def draw_radar_image_cube(key, part):
    key = jax.random.fold_in(key, 11)
    subkeys = jax.random.split(key, 4)
    common = jnp.clip(jax.random.normal(subkeys[0], (1, 2, ROWS, COLS), jnp.float32), -6.0, 6.0)
    speckle = jnp.clip(jax.random.normal(subkeys[1], (EPOCH_TOTAL, 2, ROWS, COLS), jnp.float32), -6.0, 6.0)
    correl = jax.random.uniform(subkeys[2], (EPOCH_TOTAL, 1, 1, 1), jnp.float32, 0.35, 0.95)
    texture = jnp.exp(jax.random.uniform(subkeys[3], (1, 1, ROWS, COLS), jnp.float32, -1.0, 1.0))
    mixed = correl * common + jnp.sqrt(1.0 - correl * correl) * speckle
    return (texture * mixed).astype(jnp.bfloat16)


def draw_epoch_couple_matrix(key, part):
    key = jax.random.fold_in(key, 12)
    skipped = jax.random.randint(key, (EPOCH_TOTAL,), 0, 3)
    near_off = jnp.where(skipped == 0, 2, 1)
    far_off = jnp.where(skipped == 2, 2, 3)
    offsets = jnp.stack([near_off, far_off], axis=1).reshape(-1)
    leader_epoch = jnp.arange(PAIRS, dtype=jnp.int32) // 2
    forward = leader_epoch + offsets
    follower_epoch = jnp.where(forward < EPOCH_TOTAL, forward, leader_epoch - offsets)
    return jnp.stack([leader_epoch, follower_epoch], axis=1).astype(jnp.int32)


def draw_averaged_line_grid_lines(key, part):
    key = jax.random.fold_in(key, 13)
    reach_rows = ROWS_DEV // LOOK_R
    row_index = jnp.arange(LOOK_ROWS, dtype=jnp.int32)
    offset_row = jax.random.randint(key, (LOOK_ROWS,), -reach_rows, reach_rows + 1)
    position = row_index % reach_rows
    band_odd = row_index // reach_rows % 2
    offset_row = jnp.where((position == 0) & (band_odd == 1), -reach_rows, offset_row)
    offset_row = jnp.where((position == reach_rows - 1) & (band_odd == 0), reach_rows, offset_row)
    return jnp.clip(row_index + offset_row, 0, LOOK_ROWS - 1).astype(jnp.int32)


def steps_of(key, extent, cuts, smallest, largest):
    level = 1.0
    for axis_at, blocks in cuts:
        steps = jax.random.uniform(jax.random.fold_in(jax.random.fold_in(key, 6), axis_at), (blocks,), jnp.float32, smallest / len(cuts), largest / len(cuts))
        level = level * jnp.repeat(jnp.exp(steps), extent[axis_at] // blocks).reshape((-1,) + (1,) * (len(extent) - 1 - axis_at))
    return level


def setup_inputs(seed: int = 0) -> dict:
    key_of = jax.random.split(jax.random.key(seed), 5)
    radar_image_cube = draw_radar_image_cube(jax.random.fold_in(key_of[4], 71), 0)
    orbit_separations = jnp.clip(jax.random.uniform(key_of[1], (EPOCH_TOTAL,), jnp.float32, -2.0, 2.0) * steps_of(key_of[1], (EPOCH_TOTAL,), ((0, 32),), -0.4, 0.0), -2.0, 2.0).astype(jnp.bfloat16)
    epoch_couple_matrix = draw_epoch_couple_matrix(jax.random.fold_in(key_of[4], 71), 0)
    averaged_line_grid_lines = draw_averaged_line_grid_lines(jax.random.fold_in(key_of[4], 71), 0)
    return {"radar_image_cube": radar_image_cube, "orbit_separations": orbit_separations, "epoch_couple_matrix": epoch_couple_matrix, "averaged_line_grid_lines": averaged_line_grid_lines}


phase_rate = math.pi / 64.0

def couple_averages(lead, partner, orbit_separation_step, range_angle):
    lead_real = lead[0].astype(jnp.float32)
    lead_imag = lead[1].astype(jnp.float32)
    part_real = partner[0].astype(jnp.float32)
    part_imag = partner[1].astype(jnp.float32)
    prod_real = lead_real * part_real + lead_imag * part_imag
    prod_imag = lead_imag * part_real - lead_real * part_imag
    phase_turn = orbit_separation_step * range_angle
    cosine = jnp.cos(phase_turn)[None, :]
    sine_turn = jnp.sin(phase_turn)[None, :]
    flat_real = prod_real * cosine + prod_imag * sine_turn
    flat_imag = prod_imag * cosine - prod_real * sine_turn
    lead_power = lead_real * lead_real + lead_imag * lead_imag
    part_power = part_real * part_real + part_imag * part_imag
    stacked = jnp.stack([flat_real, flat_imag, lead_power, part_power])
    row_count = stacked.shape[1]
    col_count = stacked.shape[2]
    blocked = stacked.reshape(4, row_count // LOOK_R, LOOK_R, col_count // LOOK_C, LOOK_C)
    means = lax.optimization_barrier(jnp.mean(blocked, axis=(2, 4)))
    inverse = 1.0 / jnp.sqrt(means[2] * means[3] + 1e-06)
    gamma_real = means[0] * inverse
    gamma_imag = means[1] * inverse
    coherence = jnp.sqrt(gamma_real * gamma_real + gamma_imag * gamma_imag)
    return jnp.stack([gamma_real, gamma_imag, coherence])

def reference(radar_image_cube, orbit_separations, epoch_couple_matrix, averaged_line_grid_lines):
    range_angle = jnp.arange(COLS, dtype=jnp.int32).astype(jnp.float32) * phase_rate

    def one_pair(pair_index):
        leader_epoch = epoch_couple_matrix[pair_index, 0]
        follower_epoch = epoch_couple_matrix[pair_index, 1]
        orbit_separation_step = orbit_separations[leader_epoch].astype(jnp.float32) - orbit_separations[follower_epoch].astype(jnp.float32)
        return couple_averages(radar_image_cube[leader_epoch], radar_image_cube[follower_epoch], orbit_separation_step, range_angle)
    look_stack = lax.map(one_pair, jnp.arange(PAIRS, dtype=jnp.int32))
    onehot = (averaged_line_grid_lines[:, None] == jnp.arange(LOOK_ROWS, dtype=jnp.int32)[None, :]).astype(jnp.float32)
    counts = lax.optimization_barrier(jnp.sum(onehot, axis=0))
    totals_map = jnp.einsum('pkrc,rm->pkmc', look_stack, onehot, precision=lax.Precision.HIGHEST)
    divisor = jnp.maximum(counts, 1.0)
    ifg_map = totals_map[:, 0:2] / divisor[None, None, :, None]
    coh_map = totals_map[:, 2] / divisor[None, :, None]
    return (ifg_map, coh_map)
```

```python
import math

import jax
import jax.numpy as jnp
import numpy as np
from jax import lax
from jax.experimental import pallas as pl
from jax.experimental.pallas import tpu as pltpu
from jax.sharding import PartitionSpec as P

LOOK_R = 5
LOOK_C = 20
LANES = 128
DATES = 32
SEGS = 8
TILES = 20
ROWS = 2 * TILES
DATA = LOOK_R * ROWS
CHUNK = DATA + 8
GROUPS = 4
SLOTS = 3 * DATES
TURN = 2.0 * math.pi


def two_parts(value):
    high = value.astype(jnp.bfloat16)
    low = (value - high.astype(jnp.float32)).astype(jnp.bfloat16)
    return high, low


def exact_dot(value, matrix):
    high, low = two_parts(value)
    return jnp.dot(high, matrix, preferred_element_type=jnp.float32) + jnp.dot(
        low, matrix, preferred_element_type=jnp.float32
    )


def look_kernel(
    place, lines, x, weights, out, slc, turned, base, power, cross_a, cross_b, delta, folded, partner
):
    parity = lax.broadcasted_iota(jnp.int32, (DATA, LANES), 0) % 2 == 0

    def load_date(d, _):
        block = x[d].astype(jnp.float32)
        base[pl.ds(pl.multiple_of(d * 8, 8), 8), :] = block[DATA:]
        block = block[:DATA]
        slc[d] = block
        turned[d] = jnp.where(
            parity, -pltpu.roll(block, DATA - 1, 0), pltpu.roll(block, 1, 0)
        )
        squares = block * block
        total = squares[:ROWS]
        for r in range(1, LOOK_R):
            total = total + squares[r * ROWS : (r + 1) * ROWS]
        power[pl.ds(pl.multiple_of(d * ROWS, 8), ROWS), :] = total
        return 0

    lax.fori_loop(0, DATES, load_date, 0)

    def multiply(d, _):
        for k in range(3):
            other = jnp.where(d + k + 1 < DATES, d + k + 1, d - k - 1)
            slot = k * DATES + d
            for v in range(0, ROWS, 8):
                total_a = jnp.zeros((8, LANES), jnp.float32)
                total_b = jnp.zeros((8, LANES), jnp.float32)
                for r in range(LOOK_R):
                    lead = slc[d, pl.ds(r * ROWS + v, 8), :]
                    total_a += lead * slc[other, pl.ds(r * ROWS + v, 8), :]
                    total_b += lead * turned[other, pl.ds(r * ROWS + v, 8), :]
                cross_a[pl.ds(pl.multiple_of(slot * ROWS + v, 8), 8), :] = total_a
                cross_b[pl.ds(pl.multiple_of(slot * ROWS + v, 8), 8), :] = total_b
            step = base[pl.ds(pl.multiple_of(d * 8, 8), 8), :] - base[
                pl.ds(pl.multiple_of(other * 8, 8), 8), :
            ]
            delta[pl.ds(slot * GROUPS, GROUPS), :] = step[:GROUPS]
        return 0

    lax.fori_loop(0, DATES, multiply, 0)

    block_rows = 64
    row = lax.broadcasted_iota(jnp.int32, (block_rows, LANES), 0)
    lane = lax.broadcasted_iota(jnp.int32, (block_rows, LANES), 1)
    group = row % GROUPS
    kept = (lane // 32 == group).astype(jnp.float32)
    first_tile = place[0] * TILES
    tile = (first_tile + 5 * group).astype(jnp.float32)
    within = lane.astype(jnp.float32) * (1.0 / LANES)
    summing = (
        lax.broadcasted_iota(jnp.int32, (16, block_rows), 0)
        == lax.broadcasted_iota(jnp.int32, (16, block_rows), 1) // GROUPS
    ).astype(jnp.bfloat16)

    def strided(ref, start, first):
        return ref[pl.ds(start * 10 + first, block_rows, stride=10), :]

    def gathered(value):
        high, low = two_parts(value * kept)
        return jnp.dot(summing, high, preferred_element_type=jnp.float32) + jnp.dot(
            summing, low, preferred_element_type=jnp.float32
        )

    def fold_cross(i, _):
        start = i * block_rows
        step = delta[pl.ds(pl.multiple_of(start, 8), block_rows), :]
        turns = step * tile
        turns = (turns - jnp.round(turns)) + step * within
        turns = turns - jnp.round(turns)
        angle = turns * TURN
        cosine, sine = jnp.cos(angle), jnp.sin(angle)
        once = (step - jnp.round(step)) * TURN
        turn_c, turn_s = jnp.cos(once), jnp.sin(once)
        real = jnp.zeros((block_rows, LANES), jnp.float32)
        imag = jnp.zeros((block_rows, LANES), jnp.float32)
        for k in range(5):
            prod_r = strided(cross_a, start, 2 * k) + strided(cross_a, start, 2 * k + 1)
            prod_i = strided(cross_b, start, 2 * k) + strided(cross_b, start, 2 * k + 1)
            w = weights[k]
            real += exact_dot(prod_r * cosine + prod_i * sine, w)
            imag += exact_dot(prod_i * cosine - prod_r * sine, w)
            if k < 4:
                cosine, sine = cosine * turn_c - sine * turn_s, sine * turn_c + cosine * turn_s
        folded[0, pl.ds(pl.multiple_of(i * 16, 8), 16), :] = gathered(real)
        folded[1, pl.ds(pl.multiple_of(i * 16, 8), 16), :] = gathered(imag)
        return 0

    lax.fori_loop(0, SLOTS * GROUPS // block_rows, fold_cross, 0)

    def fold_power(i, _):
        start = i * block_rows
        total = jnp.zeros((block_rows, LANES), jnp.float32)
        for k in range(5):
            both = strided(power, start, 2 * k) + strided(power, start, 2 * k + 1)
            total += exact_dot(both, weights[k])
        folded[2, pl.ds(pl.multiple_of(i * 16, 8), 16), :] = gathered(total)
        return 0

    lax.fori_loop(0, DATES * GROUPS // block_rows, fold_power, 0)

    scale = 1.0 / (LOOK_R * LOOK_C)
    lead_mean = folded[2, 0:DATES, :] * scale
    for k in range(1, 4):
        partner[0 : DATES - k, :] = folded[2, k:DATES, :]
        partner[DATES - k : DATES, :] = folded[2, DATES - 2 * k : DATES - k, :]
        part_mean = partner[...] * scale
        inverse = scale / jnp.sqrt(lead_mean * part_mean + 1e-06)
        here = pl.ds((k - 1) * DATES, DATES)
        out[pl.ds(2 * k - 2, DATES, stride=8), :] = folded[0, here, :] * inverse
        out[pl.ds(2 * k - 1, DATES, stride=8), :] = folded[1, here, :] * inverse
    line = (lines[place[1]] + 1).astype(jnp.float32)
    out[pl.ds(6, DATES, stride=8), :] = jnp.full((DATES, LANES), line, jnp.float32)
    out[pl.ds(7, DATES, stride=8), :] = jnp.zeros((DATES, LANES), jnp.float32)


def map_kernel(band, couples, below, own, above, ifg, coh):
    sources = [(ref, q) for ref in (below, own, above) for q in range(4)]
    masks = []
    counts = [jnp.zeros((8, LANES), jnp.float32) for _ in range(4)]
    for ref, q in sources:
        line = ref[pl.ds(q * 64 + 6, 8, stride=8), :]
        hit = []
        for m in range(4):
            number = (band[0] * 4 + m + 1).astype(jnp.float32)
            hit.append(line == number)
            counts[m] += hit[m].astype(jnp.float32)
        masks.append(hit)
    for pair in range(2):
        offset = jnp.abs(couples[pair, 1] - couples[pair, 0]) - 1
        sums = [[jnp.zeros((8, LANES), jnp.float32) for _ in range(4)] for _ in range(3)]
        for (ref, q), hit in zip(sources, masks):
            real = ref[pl.ds(q * 64 + 2 * offset, 8, stride=8), :]
            imag = ref[pl.ds(q * 64 + 2 * offset + 1, 8, stride=8), :]
            fields = (real, imag, jnp.sqrt(real * real + imag * imag))
            for f in range(3):
                for m in range(4):
                    sums[f][m] += jnp.where(hit[m], fields[f], 0.0)
        for m in range(4):
            divisor = jnp.maximum(counts[m], 1.0)
            for f in range(3):
                value = sums[f][m] / divisor
                for s in range(8):
                    cols = slice(s * LANES, (s + 1) * LANES)
                    if f < 2:
                        ifg[pair, f, m : m + 1, cols] = value[s : s + 1]
                    else:
                        coh[pair, m : m + 1, cols] = value[s : s + 1]


def summing_weights():
    column = np.arange(5 * LANES)
    look = np.arange(LANES) % 32
    table = (column[:, None] // LOOK_C == look[None, :]).astype(np.float32)
    return jnp.asarray(table.reshape(5, LANES, LANES), jnp.bfloat16)


def passed_along(block, axis, distance):
    devices = range(lax.axis_size(axis))
    route = [(i - distance, i) for i in devices if i - distance in devices]
    return lax.ppermute(block, axis, route)


def body(radar_image_cube, orbit_separations, epoch_couple_matrix, averaged_line_grid_lines):
    cube = radar_image_cube.reshape(2, 4, LOOK_R, SEGS, TILES, LANES)
    cube = cube.transpose(1, 3, 2, 4, 0, 5).reshape(DATES, DATA, LANES)
    tail = jnp.broadcast_to(orbit_separations.reshape(1, 1, 1), (DATES, 8, LANES))
    sent = jnp.concatenate([cube, tail], axis=1)
    got = lax.all_to_all(sent, "date", split_axis=0, concat_axis=0, tiled=True)
    me = lax.axis_index("date")
    place = jnp.stack([me % SEGS, me // SEGS]).astype(jnp.int32)
    smem = pl.BlockSpec(memory_space=pltpu.SMEM)
    vmem = pl.BlockSpec(memory_space=pltpu.VMEM)
    f32 = jnp.float32
    looks = pl.pallas_call(
        look_kernel,
        out_shape=jax.ShapeDtypeStruct((DATES * 8, LANES), f32),
        in_specs=[smem, smem, vmem, vmem],
        out_specs=vmem,
        scratch_shapes=[
            pltpu.VMEM((DATES, DATA, LANES), f32),
            pltpu.VMEM((DATES, DATA, LANES), f32),
            pltpu.VMEM((DATES * 8, LANES), f32),
            pltpu.VMEM((DATES * ROWS, LANES), f32),
            pltpu.VMEM((SLOTS * ROWS, LANES), f32),
            pltpu.VMEM((SLOTS * ROWS, LANES), f32),
            pltpu.VMEM((SLOTS * GROUPS, LANES), f32),
            pltpu.VMEM((3, SLOTS, LANES), f32),
            pltpu.VMEM((DATES, LANES), f32),
        ],
        compiler_params=pltpu.CompilerParams(vmem_limit_bytes=40 << 20),
        name="looks",
    )(place, averaged_line_grid_lines, got, summing_weights())
    own = lax.all_to_all(
        looks.reshape(DATES, 8, LANES), "date", split_axis=0, concat_axis=0, tiled=True
    ).reshape(DATES * 8, LANES)
    below = passed_along(own, "band", 1)
    above = passed_along(own, "band", -1)
    band = lax.axis_index("band").astype(jnp.int32).reshape(1)
    return pl.pallas_call(
        map_kernel,
        out_shape=(
            jax.ShapeDtypeStruct((2, 2, 4, 1024), f32),
            jax.ShapeDtypeStruct((2, 4, 1024), f32),
        ),
        in_specs=[smem, smem, vmem, vmem, vmem],
        out_specs=(vmem, vmem),
        name="map_rows",
    )(band, epoch_couple_matrix, below, own, above)


def solution(mesh):
    placed = (P("date", None, "band", None), P("date"), P("date", None), P("band"))
    return jax.shard_map(
        body,
        mesh=mesh,
        in_specs=placed,
        out_specs=(P("date", None, "band", None), P("date", "band", None)),
        check_vma=False,
    )
```

```python
import math

import jax
import jax.numpy as jnp
import numpy as np
from jax import lax
from jax.experimental import pallas as pl
from jax.experimental.pallas import tpu as pltpu
from jax.sharding import PartitionSpec as P

LOOK_R = 5
LOOK_C = 20
LANES = 128
RING = 4
LAYERS = 8
HALVES = 2
TILES = 160 // HALVES
ROWS = 2 * TILES
DATA = LOOK_R * ROWS
CHUNK = DATA + 16
GROUPS = TILES // 5
SPAN = GROUPS // 4
TURN = 2.0 * math.pi
INSIDE = ((0, 1), (0, 2), (0, 3), (1, 2), (1, 3), (2, 3))
ACROSS = ((1, 6), (4, 0), (4, 1), (5, 0), (5, 1), (5, 2))
EDGES = INSIDE + ACROSS
SLOTS = len(EDGES)
KEPT = 7
DATES = 7
FIELD = SLOTS * GROUPS
FOLD = 2 * FIELD + DATES * GROUPS


def two_parts(value):
    high = value.astype(jnp.bfloat16)
    low = (value - high.astype(jnp.float32)).astype(jnp.bfloat16)
    return high, low


def half_kernel(half, *refs):
    if half:
        lines, couples, cube, separation, out, splats = refs
    else:
        cube, separation, out = refs
    value = separation[...].astype(jnp.float32)
    tail = jnp.broadcast_to(value, (16, LANES)).astype(jnp.bfloat16)
    for q in range(RING):
        out[q, DATA:CHUNK, :] = tail
        for r in range(LOOK_R):
            first = (r * HALVES + half) * ROWS
            out[q, r * ROWS : (r + 1) * ROWS, :] = cube[q, first : first + ROWS, :]
    if half:
        line = lines[lax.axis_index("date") % RING] + 1
        splats[0:8, :] = jnp.full((8, LANES), line, jnp.int32).astype(jnp.float32)
        for pair in range(2):
            offset = jnp.abs(couples[pair, 1] - couples[pair, 0])
            here = slice(8 * pair + 8, 8 * pair + 16)
            splats[here, :] = jnp.full((8, LANES), offset, jnp.int32).astype(jnp.float32)


def look_kernel(half, got, below, above, weights, kept, lent, cross, power, terms, norm):
    parity = lax.broadcasted_iota(jnp.int32, (8, LANES), 0) % 2 == 0
    sources = [got.at[d] for d in range(4)] + [below.at[0], below.at[1], above.at[0]]

    def turned(block):
        return jnp.where(parity, -pltpu.roll(block, 7, 0), pltpu.roll(block, 1, 0))

    def products(edges, powers):
        partners = sorted({b for _, b in edges})
        used = sorted({d for e in edges for d in e})

        def step(v, _):
            sums_a = [[None, None] for _ in edges]
            sums_b = [[None, None] for _ in edges]
            squares = {d: [None, None] for d in powers}
            for r in range(LOOK_R):
                rows = pl.ds(pl.multiple_of(r * ROWS + v * 16, 16), 16)
                wide = {d: sources[d][rows, :].astype(jnp.float32) for d in used}
                for part in range(2):
                    cut = {d: wide[d][8 * part : 8 * part + 8] for d in used}
                    turn = {d: turned(cut[d]) for d in partners}
                    for i, (a, b) in enumerate(edges):
                        add_a, add_b = cut[a] * cut[b], cut[a] * turn[b]
                        sums_a[i][part] = add_a if r == 0 else sums_a[i][part] + add_a
                        sums_b[i][part] = add_b if r == 0 else sums_b[i][part] + add_b
                    for d in powers:
                        square = cut[d] * cut[d]
                        squares[d][part] = square if r == 0 else squares[d][part] + square
            for part in range(2):
                for i, e in enumerate(edges):
                    place = EDGES.index(e) * ROWS + 8 * part
                    here = pl.ds(pl.multiple_of(place + v * 16, 8), 8)
                    cross[0, here, :] = sums_a[i][part]
                    cross[1, here, :] = sums_b[i][part]
                for d in powers:
                    here = pl.ds(pl.multiple_of(d * ROWS + 8 * part + v * 16, 8), 8)
                    power[here, :] = squares[d][part]
            return 0

        lax.fori_loop(0, ROWS // 16, step, 0)

    products(INSIDE, (0, 1, 2, 3))
    products(ACROSS, (4, 5, 6))

    group = lax.broadcasted_iota(jnp.int32, (GROUPS, LANES), 0)
    lane = lax.broadcasted_iota(jnp.int32, (GROUPS, LANES), 1)
    tile = (half * TILES + 5 * group).astype(jnp.float32)
    within = lane.astype(jnp.float32) * (1.0 / LANES)

    def keep(place, k, value):
        high, low = two_parts(value)
        cols = slice(k * LANES, (k + 1) * LANES)
        terms[place : place + GROUPS, cols] = high
        terms[FOLD + place : FOLD + place + GROUPS, cols] = low

    base = [ref[DATA : DATA + 16, :].astype(jnp.float32)[:8] for ref in sources]
    for i, (a, b) in enumerate(EDGES):
        delta = base[a] - base[b]
        once = (delta - jnp.round(delta)) * TURN
        turn_c = jnp.concatenate([jnp.cos(once)] * (GROUPS // 8))
        turn_s = jnp.concatenate([jnp.sin(once)] * (GROUPS // 8))
        delta = jnp.concatenate([delta] * (GROUPS // 8))
        turns = delta * tile
        turns = (turns - jnp.round(turns)) + delta * within
        angle = (turns - jnp.round(turns)) * TURN
        cosine, sine = jnp.cos(angle), jnp.sin(angle)
        for k in range(5):
            even = pl.ds(i * ROWS + 2 * k, GROUPS, stride=10)
            odd = pl.ds(i * ROWS + 2 * k + 1, GROUPS, stride=10)
            prod_r = cross[0, even, :] + cross[0, odd, :]
            prod_i = cross[1, even, :] + cross[1, odd, :]
            keep(i * GROUPS, k, prod_r * cosine + prod_i * sine)
            keep(FIELD + i * GROUPS, k, prod_i * cosine - prod_r * sine)
            if k < 4:
                cosine, sine = cosine * turn_c - sine * turn_s, sine * turn_c + cosine * turn_s
    for d in range(DATES):
        for k in range(5):
            even = pl.ds(d * ROWS + 2 * k, GROUPS, stride=10)
            odd = pl.ds(d * ROWS + 2 * k + 1, GROUPS, stride=10)
            keep(2 * FIELD + d * GROUPS, k, power[even, :] + power[odd, :])

    summed = jnp.dot(terms[...], weights[...], preferred_element_type=jnp.float32)
    summed = summed[:FOLD] + summed[FOLD:]
    row = lax.broadcasted_iota(jnp.int32, (FOLD, LANES), 0)
    lane = lax.broadcasted_iota(jnp.int32, (FOLD, LANES), 1)
    high, low = two_parts(jnp.where(lane // 32 == row % 4, summed, 0.0))
    joined = (
        lax.broadcasted_iota(jnp.int32, (FOLD // 4, FOLD), 0)
        == lax.broadcasted_iota(jnp.int32, (FOLD // 4, FOLD), 1) // 4
    ).astype(jnp.bfloat16)
    looks = jnp.dot(joined, high, preferred_element_type=jnp.float32) + jnp.dot(
        joined, low, preferred_element_type=jnp.float32
    )
    looks = looks * (1.0 / (LOOK_R * LOOK_C))
    means = [
        looks[(2 * SLOTS + d) * SPAN : (2 * SLOTS + d + 1) * SPAN] for d in range(DATES)
    ]
    for i, (a, b) in enumerate(EDGES):
        norm[i * SPAN : (i + 1) * SPAN, :] = means[a] * means[b]
    inverse = 1.0 / jnp.sqrt(norm[...] + 1e-06)
    count = SLOTS * SPAN
    real = looks[:count] * inverse
    imag = looks[count : 2 * count] * inverse
    own = KEPT * SPAN
    rest = count - own
    kept[:own, :] = real[:own]
    kept[own:, :] = imag[:own]
    lent[:rest, :] = real[own:]
    lent[rest:, :] = imag[own:]


def gather_kernel(splats, kept0, lent0, kept1, lent1, back0, back1, out):
    last = lax.axis_index("date") // RING == LAYERS - 1
    kept, lent, back = (kept0, kept1), (lent0, lent1), (back0, back1)

    def edge(number, h, f):
        if number < KEPT:
            first = (f * KEPT + number) * SPAN
            return kept[h][first : first + SPAN, :]
        first = (f * (SLOTS - KEPT) + number - KEPT) * SPAN
        return lent[h][first : first + SPAN, :]

    def returned(number, h, f):
        first = (f * (SLOTS - KEPT) + number) * SPAN
        return back[h][first : first + SPAN, :]

    for h in range(HALVES):
        for f in range(2):

            def choose(usual, number):
                other = edge(number, h, f)
                return jnp.where(last, other if f == 0 else -other, usual)

            table = (
                (edge(0, h, f), edge(1, h, f), edge(2, h, f)),
                (edge(3, h, f), edge(4, h, f), choose(edge(6, h, f), 8)),
                (edge(5, h, f), choose(returned(0, h, f), 1), choose(returned(1, h, f), 11)),
                (
                    choose(returned(2, h, f), 5),
                    choose(returned(3, h, f), 4),
                    choose(returned(4, h, f), 2),
                ),
            )
            for x in range(RING):
                for k in range(3):
                    first = (2 * k + f) * 8 + h * SPAN
                    out[x, first : first + SPAN, :] = table[x][k]
    for x in range(RING):
        out[x, 48:56, :] = splats[0:8, :]


def map_kernel(splats, below, own, above, ifg, coh):
    sources = [(ref, q) for ref in (below, own, above) for q in range(4)]
    first = lax.axis_index("band") * 4 + 1
    masks = []
    counts = [jnp.zeros((8, LANES), jnp.float32) for _ in range(4)]
    for ref, q in sources:
        line = ref[q, 48:56, :]
        hit = []
        for m in range(4):
            hit.append(line == (first + m).astype(jnp.float32))
            counts[m] += hit[m].astype(jnp.float32)
        masks.append(hit)
    for pair in range(2):
        offset = splats[8 * pair + 8 : 8 * pair + 16, :]
        near, middle = offset == 1.0, offset == 2.0
        sums = [[jnp.zeros((8, LANES), jnp.float32) for _ in range(4)] for _ in range(3)]
        for (ref, q), hit in zip(sources, masks):

            def chosen(f):
                a, b, c = (ref[q, 16 * k + 8 * f : 16 * k + 8 * f + 8, :] for k in range(3))
                return jnp.where(near, a, jnp.where(middle, b, c))

            real, imag = chosen(0), chosen(1)
            fields = (real, imag, jnp.sqrt(real * real + imag * imag))
            for f in range(3):
                for m in range(4):
                    sums[f][m] += jnp.where(hit[m], fields[f], 0.0)
        for m in range(4):
            divisor = jnp.maximum(counts[m], 1.0)
            for f in range(3):
                value = sums[f][m] / divisor
                for s in range(8):
                    cols = slice(s * LANES, (s + 1) * LANES)
                    if f < 2:
                        ifg[pair, f, m : m + 1, cols] = value[s : s + 1]
                    else:
                        coh[pair, m : m + 1, cols] = value[s : s + 1]


def summing_weights():
    column = np.arange(5 * LANES)
    look = np.arange(LANES) % 32
    table = (column[:, None] // LOOK_C == look[None, :]).astype(np.float32)
    return jnp.asarray(table, jnp.bfloat16)


def passed_along(block, axis, distance):
    devices = range(lax.axis_size(axis))
    route = [(i - distance, i) for i in devices if i - distance in devices]
    return lax.ppermute(block, axis, route)


def moved_layers(block, step):
    route = [
        (RING * z + x, RING * ((z + step) % LAYERS) + x)
        for z in range(LAYERS)
        for x in range(RING)
    ]
    return lax.ppermute(block, "date", route)


def in_ring(block):
    rings = [[RING * z + x for x in range(RING)] for z in range(LAYERS)]
    return lax.all_to_all(
        block, "date", split_axis=0, concat_axis=0, tiled=True, axis_index_groups=rings
    )


def body(radar_image_cube, orbit_separations, epoch_couple_matrix, averaged_line_grid_lines):
    f32 = jnp.float32
    smem = pl.BlockSpec(memory_space=pltpu.SMEM)
    vmem = pl.BlockSpec(memory_space=pltpu.VMEM)
    cube = radar_image_cube.reshape(2, 20, 160, LANES)
    cube = cube.transpose(1, 2, 0, 3).reshape(RING, LOOK_R * HALVES * ROWS, LANES)
    separation = orbit_separations.reshape(1, 1)
    weights = summing_weights()
    results = []
    for h in range(HALVES):
        packed = jax.ShapeDtypeStruct((RING, CHUNK, LANES), jnp.bfloat16)
        if h:
            part, splats = pl.pallas_call(
                lambda *refs: half_kernel(1, *refs),
                out_shape=(packed, jax.ShapeDtypeStruct((24, LANES), f32)),
                in_specs=[smem, smem, vmem, vmem],
                out_specs=(vmem, vmem),
                compiler_params=pltpu.CompilerParams(vmem_limit_bytes=16 << 20),
                name="second_half",
            )(averaged_line_grid_lines, epoch_couple_matrix, cube, separation)
        else:
            part = pl.pallas_call(
                lambda *refs: half_kernel(0, *refs),
                out_shape=packed,
                in_specs=[vmem, vmem],
                out_specs=vmem,
                compiler_params=pltpu.CompilerParams(vmem_limit_bytes=16 << 20),
                name="first_half",
            )(cube, separation)
        got = in_ring(part)
        if h:
            got, above = lax.optimization_barrier((got, above))
        below = moved_layers(got[2:4], 1)
        above = moved_layers(got[0:1], -1)
        own = 2 * KEPT * SPAN
        rest = 2 * (SLOTS - KEPT) * SPAN
        kept, lent = pl.pallas_call(
            lambda *refs, h=h: look_kernel(h, *refs),
            out_shape=(
                jax.ShapeDtypeStruct((own, LANES), f32),
                jax.ShapeDtypeStruct((rest, LANES), f32),
            ),
            in_specs=[vmem] * 4,
            out_specs=(vmem, vmem),
            scratch_shapes=[
                pltpu.VMEM((2, SLOTS * ROWS, LANES), f32),
                pltpu.VMEM((DATES * ROWS, LANES), f32),
                pltpu.VMEM((2 * FOLD, 5 * LANES), jnp.bfloat16),
                pltpu.VMEM((SLOTS * SPAN, LANES), f32),
            ],
            compiler_params=pltpu.CompilerParams(vmem_limit_bytes=24 << 20),
            cost_estimate=pl.CostEstimate(
                flops=20_000_000, bytes_accessed=6_000_000, transcendentals=0
            ),
            name="looks",
        )(got, below, above, weights)
        results.append((kept, lent, moved_layers(lent, -1)))
    (kept0, lent0, back0), (kept1, lent1, back1) = results
    sent = pl.pallas_call(
        gather_kernel,
        out_shape=jax.ShapeDtypeStruct((RING, 56, LANES), f32),
        in_specs=[vmem] * 7,
        out_specs=vmem,
        compiler_params=pltpu.CompilerParams(vmem_limit_bytes=4 << 20),
        name="by_owner",
    )(splats, kept0, lent0, kept1, lent1, back0, back1)
    own = in_ring(sent)
    below = passed_along(own, "band", 1)
    above = passed_along(own, "band", -1)
    return pl.pallas_call(
        map_kernel,
        out_shape=(
            jax.ShapeDtypeStruct((2, 2, 4, 1024), f32),
            jax.ShapeDtypeStruct((2, 4, 1024), f32),
        ),
        in_specs=[vmem] * 4,
        out_specs=(vmem, vmem),
        compiler_params=pltpu.CompilerParams(vmem_limit_bytes=4 << 20),
        name="map_rows",
    )(splats, below, own, above)


def solution(mesh):
    placed = (P("date", None, "band", None), P("date"), P("date", None), P("band"))
    return jax.shard_map(
        body,
        mesh=mesh,
        in_specs=placed,
        out_specs=(P("date", None, "band", None), P("date", "band", None)),
        check_vma=False,
    )
```

```python
import math

import jax
import jax.numpy as jnp
import numpy as np
from jax import lax
from jax.experimental import pallas as pl
from jax.experimental.pallas import tpu as pltpu
from jax.sharding import PartitionSpec as P

LOOK_R = 5
LOOK_C = 20
LANES = 128
RING = 4
LAYERS = 8
TURN = 2.0 * math.pi
TILES = (120, 40)
FIRST = (0, 120)
ROWS = tuple(2 * tiles for tiles in TILES)
DATA = tuple(LOOK_R * rows for rows in ROWS)
CHUNK = tuple(data + 16 for data in DATA)
GROUPS = tuple(tiles // 5 for tiles in TILES)
SPAN = tuple(groups // 4 for groups in GROUPS)
ALL_ROWS = sum(ROWS)
INSIDE = ((0, 1), (0, 2), (0, 3), (1, 2), (1, 3), (2, 3))
ACROSS = ((1, 6), (4, 0), (4, 1), (5, 0), (5, 1), (5, 2))
ONWARD = ((1, 7), (2, 8), (2, 5), (3, 4), (3, 5), (3, 6))


def is_last():
    return lax.axis_index("date") // RING == LAYERS - 1


def two_parts(value):
    high = value.astype(jnp.bfloat16)
    low = (value - high.astype(jnp.float32)).astype(jnp.bfloat16)
    return high, low


def first_pack(cube, separation, out, raw):
    value = separation[...].astype(jnp.float32)
    tail = jnp.broadcast_to(value, (16, LANES)).astype(jnp.bfloat16)
    for part, ref in enumerate((out, raw)):
        for q in range(RING):
            ref[q, DATA[part] : CHUNK[part], :] = tail
            for r in range(LOOK_R):
                first = r * ALL_ROWS + 2 * FIRST[part]
                ref[q, r * ROWS[part] : (r + 1) * ROWS[part], :] = cube[
                    q, first : first + ROWS[part], :
                ]


def second_pack(lines, couples, raw, down, up, out, splats):
    out[:, : CHUNK[1], :] = raw[...]
    last = is_last()

    @pl.when(last)
    def _():
        out[:, CHUNK[1] :, :] = up[...]

    @pl.when(jnp.logical_not(last))
    def _():
        out[:, CHUNK[1] :, :] = down[...]

    line = lines[lax.axis_index("date") % RING] + 1
    splats[0:8, :] = jnp.full((8, LANES), line, jnp.int32).astype(jnp.float32)
    for pair in range(2):
        offset = jnp.abs(couples[pair, 1] - couples[pair, 0])
        here = slice(8 * pair + 8, 8 * pair + 16)
        splats[here, :] = jnp.full((8, LANES), offset, jnp.int32).astype(jnp.float32)


def fold_rows(part, passes):
    edges = sum(len(edges) for edges, _ in passes)
    powers = sum(len(powers) for _, powers in passes)
    rows = (2 * edges + powers) * GROUPS[part]
    return edges, powers, (rows + 15) // 16 * 16


def make_looks(part, passes, sources, weights, given, cross, power, terms, norm):
    rows_of, groups, span = ROWS[part], GROUPS[part], SPAN[part]
    edges = [e for step in passes for e in step[0]]
    dates = [d for step in passes for d in step[1]]
    _, _, fold = fold_rows(part, passes)
    parity = lax.broadcasted_iota(jnp.int32, (8, LANES), 0) % 2 == 0

    def turned(block):
        return jnp.where(parity, -pltpu.roll(block, 7, 0), pltpu.roll(block, 1, 0))

    def products(some, powers):
        partners = sorted({b for _, b in some})
        used = sorted({d for e in some for d in e} | set(powers))

        def step(v, _):
            sums_a = [[None, None] for _ in some]
            sums_b = [[None, None] for _ in some]
            squares = {d: [None, None] for d in powers}
            for r in range(LOOK_R):
                wide = {d: sources[d](r * rows_of + v * 16, 16) for d in used}
                for half in range(2):
                    cut = {d: wide[d][8 * half : 8 * half + 8] for d in used}
                    turn = {d: turned(cut[d]) for d in partners}
                    for i, (a, b) in enumerate(some):
                        add_a, add_b = cut[a] * cut[b], cut[a] * turn[b]
                        sums_a[i][half] = add_a if r == 0 else sums_a[i][half] + add_a
                        sums_b[i][half] = add_b if r == 0 else sums_b[i][half] + add_b
                    for d in powers:
                        square = cut[d] * cut[d]
                        squares[d][half] = square if r == 0 else squares[d][half] + square
            for half in range(2):
                for i, e in enumerate(some):
                    place = edges.index(e) * rows_of + 8 * half
                    here = pl.ds(pl.multiple_of(place + v * 16, 8), 8)
                    cross[0, here, :] = sums_a[i][half]
                    cross[1, here, :] = sums_b[i][half]
                for d in powers:
                    place = dates.index(d) * rows_of + 8 * half
                    here = pl.ds(pl.multiple_of(place + v * 16, 8), 8)
                    power[here, :] = squares[d][half]
            return 0

        lax.fori_loop(0, rows_of // 16, step, 0)

    for some, powers in passes:
        products(some, powers)

    group = lax.broadcasted_iota(jnp.int32, (groups, LANES), 0)
    lane = lax.broadcasted_iota(jnp.int32, (groups, LANES), 1)
    tile = (FIRST[part] + 5 * group).astype(jnp.float32)
    within = lane.astype(jnp.float32) * (1.0 / LANES)
    field = len(edges) * groups
    repeats = groups // 8

    def keep(place, k, value):
        terms[place : place + groups, k * LANES : (k + 1) * LANES] = value

    base = {d: sources[d](DATA[part], 16)[:8] for d in sorted({d for e in edges for d in e})}
    for i, (a, b) in enumerate(edges):
        delta = base[a] - base[b]
        once = (delta - jnp.round(delta)) * TURN
        turn_c = jnp.concatenate([jnp.cos(once)] * repeats)
        turn_s = jnp.concatenate([jnp.sin(once)] * repeats)
        delta = jnp.concatenate([delta] * repeats)
        turns = delta * tile
        turns = (turns - jnp.round(turns)) + delta * within
        angle = (turns - jnp.round(turns)) * TURN
        cosine, sine = jnp.cos(angle), jnp.sin(angle)
        for k in range(5):
            even = pl.ds(i * rows_of + 2 * k, groups, stride=10)
            odd = pl.ds(i * rows_of + 2 * k + 1, groups, stride=10)
            prod_r = cross[0, even, :] + cross[0, odd, :]
            prod_i = cross[1, even, :] + cross[1, odd, :]
            keep(i * groups, k, prod_r * cosine + prod_i * sine)
            keep(field + i * groups, k, prod_i * cosine - prod_r * sine)
            if k < 4:
                cosine, sine = cosine * turn_c - sine * turn_s, sine * turn_c + cosine * turn_s
    for d in range(len(dates)):
        for k in range(5):
            even = pl.ds(d * rows_of + 2 * k, groups, stride=10)
            odd = pl.ds(d * rows_of + 2 * k + 1, groups, stride=10)
            keep(2 * field + d * groups, k, power[even, :] + power[odd, :])
    filled = 2 * field + len(dates) * groups
    if fold > filled:
        terms[filled:fold, :] = jnp.zeros((fold - filled, 5 * LANES), jnp.float32)

    high, low = two_parts(terms[...])
    summed = jnp.dot(high, weights[...], preferred_element_type=jnp.float32)
    summed += jnp.dot(low, weights[...], preferred_element_type=jnp.float32)
    row = lax.broadcasted_iota(jnp.int32, (fold, LANES), 0)
    lane = lax.broadcasted_iota(jnp.int32, (fold, LANES), 1)
    high, low = two_parts(jnp.where(lane // 32 == row % 4, summed, 0.0))
    joined = (
        lax.broadcasted_iota(jnp.int32, (fold // 4, fold), 0)
        == lax.broadcasted_iota(jnp.int32, (fold // 4, fold), 1) // 4
    ).astype(jnp.bfloat16)
    looks = jnp.dot(joined, high, preferred_element_type=jnp.float32) + jnp.dot(
        joined, low, preferred_element_type=jnp.float32
    )
    looks = looks * (1.0 / (LOOK_R * LOOK_C))
    count = len(edges) * span
    means = dict(given)
    for i, d in enumerate(dates):
        first = 2 * count + i * span
        means[d] = looks[first : first + span]
    for i, (a, b) in enumerate(edges):
        norm[i * span : (i + 1) * span, :] = means[a] * means[b]
    inverse = 1.0 / jnp.sqrt(norm[...] + 1e-06)
    return looks[:count] * inverse, looks[count : 2 * count] * inverse, means


INNER = ((INSIDE, (0, 1, 2, 3)),)
OUTER = ((ACROSS, (4, 5, 6)),)
LATE = ((INSIDE, (0, 1, 2, 3)), (ONWARD, (4, 5, 6, 7, 8)))


def reader(ref, date, offset=0):
    def read(first, count):
        start = first + offset
        if not isinstance(start, int):
            start = pl.multiple_of(start, 16)
        return ref[date, pl.ds(start, count), :].astype(jnp.float32)

    return read


def inner_kernel(got, weights, gamma, powers, *scratch):
    sources = [reader(got, d) for d in range(4)]
    real, imag, means = make_looks(0, INNER, sources, weights, {}, *scratch)
    count = len(INSIDE) * SPAN[0]
    gamma[:count, :] = real
    gamma[count:, :] = imag
    for d in range(4):
        powers[d * SPAN[0] : (d + 1) * SPAN[0], :] = means[d]


def outer_kernel(got, below, above, powers, weights, kept, lent, *scratch):
    sources = [reader(got, d) for d in range(4)]
    sources += [reader(below, 0), reader(below, 1), reader(above, 0)]
    span = SPAN[0]
    given = {d: powers[d * span : (d + 1) * span, :] for d in range(4)}
    real, imag, _ = make_looks(0, OUTER, sources, weights, given, *scratch)
    kept[:span, :] = real[:span]
    kept[span:, :] = imag[:span]
    rest = (len(ACROSS) - 1) * span
    lent[:rest, :] = real[span:]
    lent[rest:, :] = imag[span:]


def late_kernel(got, weights, gamma, *scratch):
    last = is_last()
    sources = [reader(got, d) for d in range(4)]
    sources += [reader(got, d, CHUNK[1]) for d in range(3)]
    sources += [reader(got, jnp.where(last, d, 0), CHUNK[1]) for d in (2, 3)]
    real, imag, _ = make_looks(1, LATE, sources, weights, {}, *scratch)
    count = (len(INSIDE) + len(ONWARD)) * SPAN[1]
    gamma[:count, :] = real
    gamma[count:, :] = imag


def gather_kernel(splats, inner, kept, lent, back, late, out):
    last = is_last()
    count = {"inner": 6, "kept": 1, "lent": 5, "back": 5, "late": 12}
    refs = {"inner": inner, "kept": kept, "lent": lent, "back": back, "late": late}

    def edge(name, number, f):
        span = SPAN[1] if name == "late" else SPAN[0]
        first = (f * count[name] + number) * span
        return refs[name][first : first + span, :]

    def swapped(name, number, f):
        value = edge(name, number, f)
        return value if f == 0 else -value

    for f in range(2):

        def choose(usual, other):
            return jnp.where(last, other, usual)

        tables = (
            (
                tuple(edge("inner", n, f) for n in (0, 1, 2)),
                (
                    edge("inner", 3, f),
                    edge("inner", 4, f),
                    choose(edge("kept", 0, f), swapped("lent", 1, f)),
                ),
                (
                    edge("inner", 5, f),
                    choose(edge("back", 0, f), swapped("inner", 1, f)),
                    choose(edge("back", 1, f), swapped("lent", 4, f)),
                ),
                tuple(
                    choose(edge("back", n, f), swapped("inner", m, f))
                    for n, m in ((2, 5), (3, 4), (4, 2))
                ),
            ),
            (
                tuple(edge("late", n, f) for n in (0, 1, 2)),
                tuple(edge("late", n, f) for n in (3, 4, 6)),
                (
                    edge("late", 5, f),
                    choose(edge("late", 7, f), swapped("late", 1, f)),
                    choose(edge("late", 8, f), edge("late", 7, f)),
                ),
                tuple(
                    choose(edge("late", n, f), swapped("late", m, f))
                    for n, m in ((9, 5), (10, 4), (11, 2))
                ),
            ),
        )
        for part, table in enumerate(tables):
            for x in range(RING):
                for k in range(3):
                    first = (2 * k + f) * 8 + part * SPAN[0]
                    out[x, first : first + SPAN[part], :] = table[x][k]
    for x in range(RING):
        out[x, 48:56, :] = splats[0:8, :]


def map_kernel(splats, below, own, above, ifg, coh):
    sources = [(ref, q) for ref in (below, own, above) for q in range(4)]
    first = lax.axis_index("band") * 4 + 1
    masks = []
    counts = [jnp.zeros((8, LANES), jnp.float32) for _ in range(4)]
    for ref, q in sources:
        line = ref[q, 48:56, :]
        hit = []
        for m in range(4):
            hit.append(line == (first + m).astype(jnp.float32))
            counts[m] += hit[m].astype(jnp.float32)
        masks.append(hit)
    for pair in range(2):
        offset = splats[8 * pair + 8 : 8 * pair + 16, :]
        near, middle = offset == 1.0, offset == 2.0
        sums = [[jnp.zeros((8, LANES), jnp.float32) for _ in range(4)] for _ in range(3)]
        for (ref, q), hit in zip(sources, masks):

            def chosen(f):
                a, b, c = (ref[q, 16 * k + 8 * f : 16 * k + 8 * f + 8, :] for k in range(3))
                return jnp.where(near, a, jnp.where(middle, b, c))

            real, imag = chosen(0), chosen(1)
            fields = (real, imag, jnp.sqrt(real * real + imag * imag))
            for f in range(3):
                for m in range(4):
                    sums[f][m] += jnp.where(hit[m], fields[f], 0.0)
        for m in range(4):
            divisor = jnp.maximum(counts[m], 1.0)
            for f in range(3):
                value = sums[f][m] / divisor
                for s in range(8):
                    cols = slice(s * LANES, (s + 1) * LANES)
                    if f < 2:
                        ifg[pair, f, m : m + 1, cols] = value[s : s + 1]
                    else:
                        coh[pair, m : m + 1, cols] = value[s : s + 1]


def summing_weights():
    column = np.arange(5 * LANES)
    look = np.arange(LANES) % 32
    table = (column[:, None] // LOOK_C == look[None, :]).astype(np.float32)
    return jnp.asarray(table, jnp.bfloat16)


def passed_along(block, axis, distance):
    devices = range(lax.axis_size(axis))
    route = [(i - distance, i) for i in devices if i - distance in devices]
    return lax.ppermute(block, axis, route)


def moved_layers(block, step, layers=range(LAYERS)):
    route = [
        (RING * z + x, RING * (z + step) + x)
        for z in layers
        for x in range(RING)
        if z + step in range(LAYERS)
    ]
    return lax.ppermute(block, "date", route)


def in_ring(block):
    rings = [[RING * z + x for x in range(RING)] for z in range(LAYERS)]
    return lax.all_to_all(
        block, "date", split_axis=0, concat_axis=0, tiled=True, axis_index_groups=rings
    )


def looks_scratch(part, passes):
    edges, powers, fold = fold_rows(part, passes)
    f32 = jnp.float32
    return [
        pltpu.VMEM((2, edges * ROWS[part], LANES), f32),
        pltpu.VMEM((powers * ROWS[part], LANES), f32),
        pltpu.VMEM((fold, 5 * LANES), f32),
        pltpu.VMEM((edges * SPAN[part], LANES), f32),
    ]


def body(radar_image_cube, orbit_separations, epoch_couple_matrix, averaged_line_grid_lines):
    f32, bf16 = jnp.float32, jnp.bfloat16
    smem = pl.BlockSpec(memory_space=pltpu.SMEM)
    vmem = pl.BlockSpec(memory_space=pltpu.VMEM)

    def table(*shape, dtype=f32):
        return jax.ShapeDtypeStruct(shape, dtype)

    def call(kernel, outs, name, ins, scratch=(), limit=16, scalars=0, flops=0):
        return pl.pallas_call(
            kernel,
            out_shape=outs,
            in_specs=[smem] * scalars + [vmem] * (len(ins) - scalars),
            out_specs=[vmem] * len(outs),
            scratch_shapes=list(scratch),
            compiler_params=pltpu.CompilerParams(vmem_limit_bytes=limit << 20),
            cost_estimate=pl.CostEstimate(
                flops=flops, bytes_accessed=4_000_000, transcendentals=0
            ),
            name=name,
        )(*ins)

    cube = radar_image_cube.reshape(2, 20, 160, LANES)
    cube = cube.transpose(1, 2, 0, 3).reshape(RING, LOOK_R * ALL_ROWS, LANES)
    separation = orbit_separations.reshape(1, 1)
    weights = summing_weights()
    sent, raw = call(
        first_pack,
        (table(RING, CHUNK[0], LANES, dtype=bf16), table(RING, CHUNK[1], LANES, dtype=bf16)),
        "first_pack",
        (cube, separation),
    )
    got = in_ring(sent)
    down = moved_layers(raw, -1)
    up = moved_layers(raw, 1, (LAYERS - 2,))
    both, splats = call(
        second_pack,
        (table(RING, 2 * CHUNK[1], LANES, dtype=bf16), table(24, LANES)),
        "second_pack",
        (averaged_line_grid_lines, epoch_couple_matrix, raw, down, up),
        scalars=2,
    )
    got_late = in_ring(both)
    below = moved_layers(got[2:4], 1)
    above = moved_layers(got[0:1], -1)
    inner, powers = call(
        inner_kernel,
        (table(12 * SPAN[0], LANES), table(4 * SPAN[0], LANES)),
        "inner_looks",
        (got, weights),
        looks_scratch(0, INNER),
        24,
        flops=10_000_000,
    )
    kept, lent = call(
        outer_kernel,
        (table(2 * SPAN[0], LANES), table(10 * SPAN[0], LANES)),
        "outer_looks",
        (got, below, above, powers, weights),
        looks_scratch(0, OUTER),
        24,
        flops=10_000_000,
    )
    back = moved_layers(lent, -1)
    (late,) = call(
        late_kernel,
        (table(24 * SPAN[1], LANES),),
        "late_looks",
        (got_late, weights),
        looks_scratch(1, LATE),
        24,
        flops=10_000_000,
    )
    (by_owner,) = call(
        gather_kernel,
        (table(RING, 56, LANES),),
        "by_owner",
        (splats, inner, kept, lent, back, late),
        limit=4,
    )
    own = in_ring(by_owner)
    below = passed_along(own, "band", 1)
    above = passed_along(own, "band", -1)
    return tuple(
        call(
            map_kernel,
            (table(2, 2, 4, 1024), table(2, 4, 1024)),
            "map_rows",
            (splats, below, own, above),
            limit=4,
        )
    )


def solution(mesh):
    placed = (P("date", None, "band", None), P("date"), P("date", None), P("band"))
    return jax.shard_map(
        body,
        mesh=mesh,
        in_specs=placed,
        out_specs=(P("date", None, "band", None), P("date", "band", None)),
        check_vma=False,
    )
```

```python
import math

import jax
import jax.numpy as jnp
import numpy as np
from jax import lax
from jax.experimental import pallas as pl
from jax.experimental.pallas import tpu as pltpu
from jax.sharding import PartitionSpec as P

LOOK_R = 5
LOOK_C = 20
LANES = 128
RING = 4
LAYERS = 8
TURN = 2.0 * math.pi
TILES = (120, 40)
FIRST = (0, TILES[0])
USED = tuple(2 * tiles for tiles in TILES)
ROWS = tuple((used + 15) // 16 * 16 for used in USED)
DATA = tuple(LOOK_R * rows for rows in ROWS)
CHUNK = tuple(data + 16 for data in DATA)
GROUPS = tuple(tiles // 5 for tiles in TILES)
SPAN = tuple(groups // 4 for groups in GROUPS)
ALL_ROWS = sum(USED)
INSIDE = ((0, 1), (0, 2), (0, 3), (1, 2), (1, 3), (2, 3))
ONWARD = ((1, 4), (2, 4), (2, 5), (3, 4), (3, 5), (3, 6))
BACKWARD = (((1, 7), (1, 4)), ((2, 8), (2, 4)))
INSTEAD = {7: 4, 8: 5}


def is_last():
    return lax.axis_index("date") // RING == LAYERS - 1


def two_parts(value):
    high = value.astype(jnp.bfloat16)
    low = (value - high.astype(jnp.float32)).astype(jnp.bfloat16)
    return high, low


def first_pack(cube, separation, out, raw):
    value = separation[...].astype(jnp.float32)
    tail = jnp.broadcast_to(value, (16, LANES)).astype(jnp.bfloat16)
    for part, ref in enumerate((out, raw)):
        for q in range(RING):
            ref[q, DATA[part] : CHUNK[part], :] = tail
            for r in range(LOOK_R):
                first = r * ALL_ROWS + 2 * FIRST[part]
                block = cube[q, first : first + USED[part], :]
                if ROWS[part] > USED[part]:
                    more = jnp.zeros((ROWS[part] - USED[part], LANES), jnp.bfloat16)
                    block = jnp.concatenate([block, more])
                ref[q, r * ROWS[part] : (r + 1) * ROWS[part], :] = block


def second_pack(lines, couples, raw, down, up, out, splats):
    out[:, : CHUNK[1], :] = raw[...]
    last = is_last()

    @pl.when(last)
    def _():
        out[:, CHUNK[1] :, :] = up[...]

    @pl.when(jnp.logical_not(last))
    def _():
        out[:, CHUNK[1] :, :] = down[...]

    line = lines[lax.axis_index("date") % RING] + 1
    splats[0:8, :] = jnp.full((8, LANES), line, jnp.int32).astype(jnp.float32)
    for pair in range(2):
        offset = jnp.abs(couples[pair, 1] - couples[pair, 0])
        here = slice(8 * pair + 8, 8 * pair + 16)
        splats[here, :] = jnp.full((8, LANES), offset, jnp.int32).astype(jnp.float32)


def fold_rows(part, passes):
    edges = sum(len(edges) for edges, _ in passes)
    powers = sum(len(powers) for _, powers in passes)
    rows = (2 * edges + powers) * GROUPS[part]
    return edges, powers, (rows + 15) // 16 * 16


def make_looks(part, passes, sources, weights, given, cross, power, terms, norm):
    rows_of, groups, span = ROWS[part], GROUPS[part], SPAN[part]
    edges = [e for step in passes for e in step[0]]
    dates = [d for step in passes for d in step[1]]
    _, _, fold = fold_rows(part, passes)
    parity = lax.broadcasted_iota(jnp.int32, (8, LANES), 0) % 2 == 0

    def turned(block):
        return jnp.where(parity, -pltpu.roll(block, 7, 0), pltpu.roll(block, 1, 0))

    def products(some, powers, edge_place, power_place):
        partners = sorted({b for _, b in some})
        used = sorted({d for e in some for d in e} | set(powers))

        def step(v, _):
            sums_a = [[None, None] for _ in some]
            sums_b = [[None, None] for _ in some]
            squares = {d: [None, None] for d in powers}
            for r in range(LOOK_R):
                wide = {d: sources[d](r * rows_of + v * 16, 16) for d in used}
                for half in range(2):
                    cut = {d: wide[d][8 * half : 8 * half + 8] for d in used}
                    turn = {d: turned(cut[d]) for d in partners}
                    for i, (a, b) in enumerate(some):
                        add_a, add_b = cut[a] * cut[b], cut[a] * turn[b]
                        sums_a[i][half] = add_a if r == 0 else sums_a[i][half] + add_a
                        sums_b[i][half] = add_b if r == 0 else sums_b[i][half] + add_b
                    for d in powers:
                        square = cut[d] * cut[d]
                        squares[d][half] = square if r == 0 else squares[d][half] + square
            for half in range(2):
                for i in range(len(some)):
                    place = edge_place[i] * rows_of + 8 * half
                    here = pl.ds(pl.multiple_of(place + v * 16, 8), 8)
                    cross[0, here, :] = sums_a[i][half]
                    cross[1, here, :] = sums_b[i][half]
                for i, d in enumerate(powers):
                    place = power_place[i] * rows_of + 8 * half
                    here = pl.ds(pl.multiple_of(place + v * 16, 8), 8)
                    power[here, :] = squares[d][half]
            return 0

        lax.fori_loop(0, rows_of // 16, step, 0)

    def run(some, powers):
        products(some, powers, [edges.index(e) for e in some], [dates.index(d) for d in powers])

    last = is_last()
    for some, powers in passes:
        if some != ONWARD:
            run(some, powers)
            continue

        @pl.when(jnp.logical_not(last))
        def _():
            run(some, powers)

        @pl.when(last)
        def _():
            wanted = [e for _, e in BACKWARD]
            products(
                [e for e, _ in BACKWARD],
                list(INSTEAD),
                [edges.index(e) for e in wanted],
                [dates.index(d) for d in INSTEAD.values()],
            )
            nothing = jnp.zeros((rows_of, LANES), jnp.float32)
            for e in some:
                if e not in wanted:
                    here = slice(edges.index(e) * rows_of, (edges.index(e) + 1) * rows_of)
                    cross[0, here, :] = nothing
                    cross[1, here, :] = nothing
            for d in powers:
                if d not in INSTEAD.values():
                    power[dates.index(d) * rows_of : (dates.index(d) + 1) * rows_of, :] = nothing

    group = lax.broadcasted_iota(jnp.int32, (groups, LANES), 0)
    lane = lax.broadcasted_iota(jnp.int32, (groups, LANES), 1)
    tile = (FIRST[part] + 5 * group).astype(jnp.float32)
    within = lane.astype(jnp.float32) * (1.0 / LANES)
    field = len(edges) * groups
    repeats = (groups + 7) // 8

    def keep(place, k, value):
        terms[place : place + groups, k * LANES : (k + 1) * LANES] = value

    base = [read(DATA[part], 16)[:8] for read in sources]
    instead = {e: d for (_, d), e in BACKWARD} if ONWARD[0] in edges else {}
    for i, (a, b) in enumerate(edges):
        other = base[b]
        if (a, b) in instead:
            other = jnp.where(last, base[instead[a, b]], other)
        delta = base[a] - other
        once = (delta - jnp.round(delta)) * TURN
        turn_c = jnp.concatenate([jnp.cos(once)] * repeats)[:groups]
        turn_s = jnp.concatenate([jnp.sin(once)] * repeats)[:groups]
        delta = jnp.concatenate([delta] * repeats)[:groups]
        turns = delta * tile
        turns = (turns - jnp.round(turns)) + delta * within
        angle = (turns - jnp.round(turns)) * TURN
        cosine, sine = jnp.cos(angle), jnp.sin(angle)
        for k in range(5):
            even = pl.ds(i * rows_of + 2 * k, groups, stride=10)
            odd = pl.ds(i * rows_of + 2 * k + 1, groups, stride=10)
            prod_r = cross[0, even, :] + cross[0, odd, :]
            prod_i = cross[1, even, :] + cross[1, odd, :]
            keep(i * groups, k, prod_r * cosine + prod_i * sine)
            keep(field + i * groups, k, prod_i * cosine - prod_r * sine)
            if k < 4:
                cosine, sine = cosine * turn_c - sine * turn_s, sine * turn_c + cosine * turn_s
    for d in range(len(dates)):
        for k in range(5):
            even = pl.ds(d * rows_of + 2 * k, groups, stride=10)
            odd = pl.ds(d * rows_of + 2 * k + 1, groups, stride=10)
            keep(2 * field + d * groups, k, power[even, :] + power[odd, :])
    filled = 2 * field + len(dates) * groups
    if fold > filled:
        terms[filled:fold, :] = jnp.zeros((fold - filled, 5 * LANES), jnp.float32)

    high, low = two_parts(terms[...])
    summed = jnp.dot(high, weights[...], preferred_element_type=jnp.float32)
    summed += jnp.dot(low, weights[...], preferred_element_type=jnp.float32)
    row = lax.broadcasted_iota(jnp.int32, (fold, LANES), 0)
    lane = lax.broadcasted_iota(jnp.int32, (fold, LANES), 1)
    high, low = two_parts(jnp.where(lane // 32 == row % 4, summed, 0.0))
    joined = (
        lax.broadcasted_iota(jnp.int32, (fold // 4, fold), 0)
        == lax.broadcasted_iota(jnp.int32, (fold // 4, fold), 1) // 4
    ).astype(jnp.bfloat16)
    looks = jnp.dot(joined, high, preferred_element_type=jnp.float32) + jnp.dot(
        joined, low, preferred_element_type=jnp.float32
    )
    looks = looks * (1.0 / (LOOK_R * LOOK_C))
    count = len(edges) * span
    means = dict(given)
    for i, d in enumerate(dates):
        first = 2 * count + i * span
        means[d] = looks[first : first + span]
    for i, (a, b) in enumerate(edges):
        other = means[b]
        if (a, b) in instead:
            other = jnp.where(last, means[INSTEAD[instead[a, b]]], other)
        norm[i * span : (i + 1) * span, :] = means[a] * other
    inverse = 1.0 / jnp.sqrt(norm[...] + 1e-06)
    return looks[:count] * inverse, looks[count : 2 * count] * inverse, means


INNER = ((INSIDE, (0, 1, 2, 3)),)
OUTER = ((ONWARD, (4, 5, 6)),)
LATE = ((INSIDE, (0, 1, 2, 3)), (ONWARD, (4, 5, 6)))


def reader(ref, date, offset=0):
    def read(first, count):
        start = first + offset
        if not isinstance(start, int):
            start = pl.multiple_of(start, 16)
        return ref[date, pl.ds(start, count), :].astype(jnp.float32)

    return read


def inner_kernel(got, weights, gamma, powers, *scratch):
    sources = [reader(got, d) for d in range(4)]
    real, imag, means = make_looks(0, INNER, sources, weights, {}, *scratch)
    count = len(INSIDE) * SPAN[0]
    gamma[:count, :] = real
    gamma[count:, :] = imag
    for d in range(4):
        powers[d * SPAN[0] : (d + 1) * SPAN[0], :] = means[d]


def outer_kernel(got, down, powers, weights, up_far, gamma, up, sem, *scratch):
    last = is_last()

    @pl.when(last)
    def _():
        copy = pltpu.make_async_copy(up_far, up, sem)
        copy.start()
        copy.wait()

    @pl.when(jnp.logical_not(last))
    def _():
        up[:, DATA[0] :, :] = jnp.zeros((2, 16, LANES), jnp.bfloat16)

    sources = [reader(got, d) for d in range(4)] + [reader(down, d) for d in range(3)]
    sources += [reader(up, d) for d in range(2)]
    span = SPAN[0]
    given = {d: powers[d * span : (d + 1) * span, :] for d in range(4)}
    real, imag, _ = make_looks(0, OUTER, sources, weights, given, *scratch)
    count = len(ONWARD) * span
    gamma[:count, :] = real
    gamma[count:, :] = imag


def late_kernel(got, weights, gamma, *scratch):
    sources = [reader(got, d) for d in range(4)]
    sources += [reader(got, d, CHUNK[1]) for d in (0, 1, 2, 2, 3)]
    real, imag, _ = make_looks(1, LATE, sources, weights, {}, *scratch)
    count = (len(INSIDE) + len(ONWARD)) * SPAN[1]
    gamma[:count, :] = real
    gamma[count:, :] = imag


def gather_kernel(splats, inner, outer, late, out):
    last = is_last()

    def edge(part, number, f):
        if part:
            ref, number, count = late, number, len(INSIDE) + len(ONWARD)
        elif number < len(INSIDE):
            ref, count = inner, len(INSIDE)
        else:
            ref, number, count = outer, number - len(INSIDE), len(ONWARD)
        first = (f * count + number) * SPAN[part]
        return ref[first : first + SPAN[part], :]

    for part in range(2):
        for f in range(2):

            def either_of(usual, other, swap=True):
                there = edge(part, other, f)
                if swap and f:
                    there = -there
                return jnp.where(last, there, edge(part, usual, f))

            table = (
                tuple(edge(part, n, f) for n in (0, 1, 2)),
                tuple(edge(part, n, f) for n in (3, 4, 6)),
                (edge(part, 5, f), either_of(7, 1), either_of(8, 7, swap=False)),
                (either_of(9, 5), either_of(10, 4), either_of(11, 2)),
            )
            for x in range(RING):
                for k in range(3):
                    first = (2 * k + f) * 8 + part * SPAN[0]
                    out[x, first : first + SPAN[part], :] = table[x][k]
    for x in range(RING):
        out[x, 48:56, :] = splats[0:8, :]


def map_kernel(splats, below, own, above, ifg, coh):
    sources = [(ref, q) for ref in (below, own, above) for q in range(4)]
    first = lax.axis_index("band") * 4 + 1
    masks = []
    counts = [jnp.zeros((8, LANES), jnp.float32) for _ in range(4)]
    for ref, q in sources:
        line = ref[q, 48:56, :]
        hit = []
        for m in range(4):
            hit.append(line == (first + m).astype(jnp.float32))
            counts[m] += hit[m].astype(jnp.float32)
        masks.append(hit)
    for pair in range(2):
        offset = splats[8 * pair + 8 : 8 * pair + 16, :]
        near, middle = offset == 1.0, offset == 2.0
        sums = [[jnp.zeros((8, LANES), jnp.float32) for _ in range(4)] for _ in range(3)]
        for (ref, q), hit in zip(sources, masks):

            def chosen(f):
                a, b, c = (ref[q, 16 * k + 8 * f : 16 * k + 8 * f + 8, :] for k in range(3))
                return jnp.where(near, a, jnp.where(middle, b, c))

            real, imag = chosen(0), chosen(1)
            fields = (real, imag, jnp.sqrt(real * real + imag * imag))
            for f in range(3):
                for m in range(4):
                    sums[f][m] += jnp.where(hit[m], fields[f], 0.0)
        for m in range(4):
            divisor = jnp.maximum(counts[m], 1.0)
            for f in range(3):
                value = sums[f][m] / divisor
                for s in range(8):
                    cols = slice(s * LANES, (s + 1) * LANES)
                    if f < 2:
                        ifg[pair, f, m : m + 1, cols] = value[s : s + 1]
                    else:
                        coh[pair, m : m + 1, cols] = value[s : s + 1]


def summing_weights():
    column = np.arange(5 * LANES)
    look = np.arange(LANES) % 32
    table = (column[:, None] // LOOK_C == look[None, :]).astype(np.float32)
    return jnp.asarray(table, jnp.bfloat16)


def passed_along(block, axis, distance):
    devices = range(lax.axis_size(axis))
    route = [(i - distance, i) for i in devices if i - distance in devices]
    return lax.ppermute(block, axis, route)


def moved_layers(block, step, layers=range(LAYERS)):
    route = [
        (RING * z + x, RING * (z + step) + x)
        for z in layers
        for x in range(RING)
        if z + step in range(LAYERS)
    ]
    return lax.ppermute(block, "date", route)


def in_ring(block):
    rings = [[RING * z + x for x in range(RING)] for z in range(LAYERS)]
    return lax.all_to_all(
        block, "date", split_axis=0, concat_axis=0, tiled=True, axis_index_groups=rings
    )


def looks_scratch(part, passes):
    edges, powers, fold = fold_rows(part, passes)
    f32 = jnp.float32
    return [
        pltpu.VMEM((2, edges * ROWS[part], LANES), f32),
        pltpu.VMEM((powers * ROWS[part], LANES), f32),
        pltpu.VMEM((fold, 5 * LANES), f32),
        pltpu.VMEM((edges * SPAN[part], LANES), f32),
    ]


def body(radar_image_cube, orbit_separations, epoch_couple_matrix, averaged_line_grid_lines):
    f32, bf16 = jnp.float32, jnp.bfloat16
    smem = pl.BlockSpec(memory_space=pltpu.SMEM)
    vmem = pl.BlockSpec(memory_space=pltpu.VMEM)
    hbm = pl.BlockSpec(memory_space=pltpu.HBM)

    def table(*shape, dtype=f32):
        return jax.ShapeDtypeStruct(shape, dtype)

    def call(kernel, outs, name, ins, scratch=(), limit=8, scalars=0, flops=0, far=0):
        return pl.pallas_call(
            kernel,
            out_shape=outs,
            in_specs=[smem] * scalars + [vmem] * (len(ins) - scalars - far) + [hbm] * far,
            out_specs=[vmem] * len(outs),
            scratch_shapes=list(scratch),
            compiler_params=pltpu.CompilerParams(vmem_limit_bytes=limit << 20),
            cost_estimate=pl.CostEstimate(
                flops=flops, bytes_accessed=4_000_000, transcendentals=0
            ),
            name=name,
        )(*ins)

    cube = radar_image_cube.reshape(2, 20, 160, LANES)
    cube = cube.transpose(1, 2, 0, 3).reshape(RING, LOOK_R * ALL_ROWS, LANES)
    separation = orbit_separations.reshape(1, 1)
    weights = summing_weights()
    sent, raw = call(
        first_pack,
        (table(RING, CHUNK[0], LANES, dtype=bf16), table(RING, CHUNK[1], LANES, dtype=bf16)),
        "first_pack",
        (cube, separation),
    )
    got = in_ring(sent)
    down = moved_layers(raw, -1)
    up = moved_layers(raw, 1, (LAYERS - 2,))
    both, splats = call(
        second_pack,
        (table(RING, 2 * CHUNK[1], LANES, dtype=bf16), table(24, LANES)),
        "second_pack",
        (averaged_line_grid_lines, epoch_couple_matrix, raw, down, up),
        scalars=2,
    )
    got_late = in_ring(both)
    onward = moved_layers(got[0:3], -1)
    backward = moved_layers(got[2:4], 1, (LAYERS - 2,))
    inner, powers = call(
        inner_kernel,
        (table(12 * SPAN[0], LANES), table(4 * SPAN[0], LANES)),
        "inner_looks",
        (got, weights),
        looks_scratch(0, INNER),
        12,
        flops=10_000_000,
    )
    (outer,) = call(
        outer_kernel,
        (table(12 * SPAN[0], LANES),),
        "outer_looks",
        (got, onward, powers, weights, backward),
        [pltpu.VMEM((2, CHUNK[0], LANES), bf16), pltpu.SemaphoreType.DMA]
        + looks_scratch(0, OUTER),
        12,
        flops=10_000_000,
        far=1,
    )
    (late,) = call(
        late_kernel,
        (table(24 * SPAN[1], LANES),),
        "late_looks",
        (got_late, weights),
        looks_scratch(1, LATE),
        12,
        flops=10_000_000,
    )
    (by_owner,) = call(
        gather_kernel,
        (table(RING, 56, LANES),),
        "by_owner",
        (splats, inner, outer, late),
        limit=4,
    )
    own = in_ring(by_owner)
    below = passed_along(own, "band", 1)
    above = passed_along(own, "band", -1)
    return tuple(
        call(
            map_kernel,
            (table(2, 2, 4, 1024), table(2, 4, 1024)),
            "map_rows",
            (splats, below, own, above),
            limit=4,
        )
    )


def solution(mesh):
    placed = (P("date", None, "band", None), P("date"), P("date", None), P("band"))
    return jax.shard_map(
        body,
        mesh=mesh,
        in_specs=placed,
        out_specs=(P("date", None, "band", None), P("date", "band", None)),
        check_vma=False,
    )
```

```python
import math

import jax
import jax.numpy as jnp
import numpy as np
from jax import lax
from jax.experimental import pallas as pl
from jax.experimental.pallas import tpu as pltpu
from jax.sharding import PartitionSpec as P

LOOK_R = 5
LOOK_C = 20
LANES = 128
RING = 4
LAYERS = 8
TURN = 2.0 * math.pi
TILES = (120, 40)
FIRST = (0, TILES[0])
USED = tuple(2 * tiles for tiles in TILES)
ROWS = tuple((used + 15) // 16 * 16 for used in USED)
DATA = tuple(LOOK_R * rows for rows in ROWS)
CHUNK = tuple(data + 16 for data in DATA)
GROUPS = tuple(tiles // 5 for tiles in TILES)
SPAN = tuple(groups // 4 for groups in GROUPS)
ALL_ROWS = sum(USED)
INSIDE = ((0, 1), (0, 2), (0, 3), (1, 2), (1, 3), (2, 3))
ONWARD = ((1, 4), (2, 4), (2, 5), (3, 4), (3, 5), (3, 6))
TURNED = ((1, 4), (2, 5))
BACKWARD = (((1, 7), (1, 4)), ((2, 8), (2, 4)))
INSTEAD = {7: 4, 8: 5}


def is_last():
    return lax.axis_index("date") // RING == LAYERS - 1


def two_parts(value):
    high = value.astype(jnp.bfloat16)
    low = (value - high.astype(jnp.float32)).astype(jnp.bfloat16)
    return high, low


def first_pack(cube, separation, out, raw):
    value = separation[...].astype(jnp.float32)
    tail = jnp.broadcast_to(value, (16, LANES)).astype(jnp.bfloat16)
    for part, ref in enumerate((out, raw)):
        for q in range(RING):
            ref[q, DATA[part] : CHUNK[part], :] = tail
            for r in range(LOOK_R):
                first = r * ALL_ROWS + 2 * FIRST[part]
                block = cube[q, first : first + USED[part], :]
                if ROWS[part] > USED[part]:
                    more = jnp.zeros((ROWS[part] - USED[part], LANES), jnp.bfloat16)
                    block = jnp.concatenate([block, more])
                ref[q, r * ROWS[part] : (r + 1) * ROWS[part], :] = block


def second_pack(lines, couples, raw, down, up, out, splats):
    out[:, : CHUNK[1], :] = raw[...]
    last = is_last()

    @pl.when(last)
    def _():
        out[:, CHUNK[1] :, :] = up[...]

    @pl.when(jnp.logical_not(last))
    def _():
        out[:, CHUNK[1] :, :] = down[...]

    line = lines[lax.axis_index("date") % RING] + 1
    splats[0:8, :] = jnp.full((8, LANES), line, jnp.int32).astype(jnp.float32)
    for pair in range(2):
        offset = jnp.abs(couples[pair, 1] - couples[pair, 0])
        here = slice(8 * pair + 8, 8 * pair + 16)
        splats[here, :] = jnp.full((8, LANES), offset, jnp.int32).astype(jnp.float32)


def fold_rows(part, passes):
    edges = sum(len(edges) for edges, _ in passes)
    powers = sum(len(powers) for _, powers in passes)
    rows = (2 * edges + powers) * GROUPS[part]
    return edges, powers, (rows + 15) // 16 * 16


def make_looks(part, passes, sources, weights, given, swap, cross, power, terms, norm):
    rows_of, groups, span = ROWS[part], GROUPS[part], SPAN[part]
    edges = [e for step in passes for e in step[0]]
    dates = [d for step in passes for d in step[1]]
    _, _, fold = fold_rows(part, passes)
    parity = lax.broadcasted_iota(jnp.int32, (8, LANES), 0) % 2 == 0

    def turned(block):
        return jnp.where(parity, -pltpu.roll(block, 7, 0), pltpu.roll(block, 1, 0))

    def products(some, powers, edge_place, power_place):
        partners = sorted({b for _, b in some})
        used = sorted({d for e in some for d in e} | set(powers))

        def step(v, _):
            sums_a = [[None, None] for _ in some]
            sums_b = [[None, None] for _ in some]
            squares = {d: [None, None] for d in powers}
            for r in range(LOOK_R):
                wide = {d: sources[d](r * rows_of + v * 16, 16) for d in used}
                for half in range(2):
                    cut = {d: wide[d][8 * half : 8 * half + 8] for d in used}
                    turn = {d: turned(cut[d]) for d in partners}
                    for i, (a, b) in enumerate(some):
                        add_a, add_b = cut[a] * cut[b], cut[a] * turn[b]
                        sums_a[i][half] = add_a if r == 0 else sums_a[i][half] + add_a
                        sums_b[i][half] = add_b if r == 0 else sums_b[i][half] + add_b
                    for d in powers:
                        square = cut[d] * cut[d]
                        squares[d][half] = square if r == 0 else squares[d][half] + square
            for half in range(2):
                for i in range(len(some)):
                    place = edge_place[i] * rows_of + 8 * half
                    here = pl.ds(pl.multiple_of(place + v * 16, 8), 8)
                    cross[0, here, :] = sums_a[i][half]
                    cross[1, here, :] = sums_b[i][half]
                for i, d in enumerate(powers):
                    place = power_place[i] * rows_of + 8 * half
                    here = pl.ds(pl.multiple_of(place + v * 16, 8), 8)
                    power[here, :] = squares[d][half]
            return 0

        lax.fori_loop(0, rows_of // 16, step, 0)

    def run(some, powers):
        products(some, powers, [edges.index(e) for e in some], [dates.index(d) for d in powers])

    last = is_last()
    for some, powers in passes:
        if not swap or some != ONWARD:
            run(some, powers)
            continue

        @pl.when(jnp.logical_not(last))
        def _():
            run(some, powers)

        @pl.when(last)
        def _():
            wanted = [e for _, e in BACKWARD]
            products(
                [e for e, _ in BACKWARD],
                list(INSTEAD),
                [edges.index(e) for e in wanted],
                [dates.index(d) for d in INSTEAD.values()],
            )
            nothing = jnp.zeros((rows_of, LANES), jnp.float32)
            for e in some:
                if e not in wanted:
                    here = slice(edges.index(e) * rows_of, (edges.index(e) + 1) * rows_of)
                    cross[0, here, :] = nothing
                    cross[1, here, :] = nothing
            for d in powers:
                if d not in INSTEAD.values():
                    power[dates.index(d) * rows_of : (dates.index(d) + 1) * rows_of, :] = nothing

    group = lax.broadcasted_iota(jnp.int32, (groups, LANES), 0)
    lane = lax.broadcasted_iota(jnp.int32, (groups, LANES), 1)
    tile = (FIRST[part] + 5 * group).astype(jnp.float32)
    within = lane.astype(jnp.float32) * (1.0 / LANES)
    field = len(edges) * groups
    repeats = (groups + 7) // 8

    def keep(place, k, value):
        terms[place : place + groups, k * LANES : (k + 1) * LANES] = value

    base = [read and read(DATA[part], 16)[:8] for read in sources]
    instead = {e: d for (_, d), e in BACKWARD} if swap else {}
    for i, (a, b) in enumerate(edges):
        other = base[b]
        if (a, b) in instead:
            other = jnp.where(last, base[instead[a, b]], other)
        delta = base[a] - other
        once = (delta - jnp.round(delta)) * TURN
        turn_c = jnp.concatenate([jnp.cos(once)] * repeats)[:groups]
        turn_s = jnp.concatenate([jnp.sin(once)] * repeats)[:groups]
        delta = jnp.concatenate([delta] * repeats)[:groups]
        turns = delta * tile
        turns = (turns - jnp.round(turns)) + delta * within
        angle = (turns - jnp.round(turns)) * TURN
        cosine, sine = jnp.cos(angle), jnp.sin(angle)
        for k in range(5):
            even = pl.ds(i * rows_of + 2 * k, groups, stride=10)
            odd = pl.ds(i * rows_of + 2 * k + 1, groups, stride=10)
            prod_r = cross[0, even, :] + cross[0, odd, :]
            prod_i = cross[1, even, :] + cross[1, odd, :]
            keep(i * groups, k, prod_r * cosine + prod_i * sine)
            keep(field + i * groups, k, prod_i * cosine - prod_r * sine)
            if k < 4:
                cosine, sine = cosine * turn_c - sine * turn_s, sine * turn_c + cosine * turn_s
    for d in range(len(dates)):
        for k in range(5):
            even = pl.ds(d * rows_of + 2 * k, groups, stride=10)
            odd = pl.ds(d * rows_of + 2 * k + 1, groups, stride=10)
            keep(2 * field + d * groups, k, power[even, :] + power[odd, :])
    filled = 2 * field + len(dates) * groups
    if fold > filled:
        terms[filled:fold, :] = jnp.zeros((fold - filled, 5 * LANES), jnp.float32)

    high, low = two_parts(terms[...])
    summed = jnp.dot(high, weights[...], preferred_element_type=jnp.float32)
    summed += jnp.dot(low, weights[...], preferred_element_type=jnp.float32)
    row = lax.broadcasted_iota(jnp.int32, (fold, LANES), 0)
    lane = lax.broadcasted_iota(jnp.int32, (fold, LANES), 1)
    high, low = two_parts(jnp.where(lane // 32 == row % 4, summed, 0.0))
    joined = (
        lax.broadcasted_iota(jnp.int32, (fold // 4, fold), 0)
        == lax.broadcasted_iota(jnp.int32, (fold // 4, fold), 1) // 4
    ).astype(jnp.bfloat16)
    looks = jnp.dot(joined, high, preferred_element_type=jnp.float32) + jnp.dot(
        joined, low, preferred_element_type=jnp.float32
    )
    looks = looks * (1.0 / (LOOK_R * LOOK_C))
    count = len(edges) * span
    means = dict(given)
    for i, d in enumerate(dates):
        first = 2 * count + i * span
        means[d] = looks[first : first + span]
    for i, (a, b) in enumerate(edges):
        other = means[b]
        if (a, b) in instead:
            other = jnp.where(last, means[INSTEAD[instead[a, b]]], other)
        norm[i * span : (i + 1) * span, :] = means[a] * other
    inverse = 1.0 / jnp.sqrt(norm[...] + 1e-06)
    return looks[:count] * inverse, looks[count : 2 * count] * inverse, means


INNER = ((INSIDE, (0, 1, 2, 3)),)
OUTER = ((ONWARD, (4, 5, 6)),)
TURN_BACK = ((TURNED, (4, 5)),)
LATE = ((INSIDE, (0, 1, 2, 3)), (ONWARD, (4, 5, 6)))


def reader(ref, date, offset=0):
    def read(first, count):
        start = first + offset
        if not isinstance(start, int):
            start = pl.multiple_of(start, 16)
        return ref[date, pl.ds(start, count), :].astype(jnp.float32)

    return read


def inner_kernel(got, weights, gamma, powers, *scratch):
    sources = [reader(got, d) for d in range(4)]
    real, imag, means = make_looks(0, INNER, sources, weights, {}, False, *scratch)
    count = len(INSIDE) * SPAN[0]
    gamma[:count, :] = real
    gamma[count:, :] = imag
    for d in range(4):
        powers[d * SPAN[0] : (d + 1) * SPAN[0], :] = means[d]


def outer_kernel(got, down, powers, weights, gamma, *scratch):
    last = is_last()
    span = SPAN[0]
    count = len(ONWARD) * span

    @pl.when(jnp.logical_not(last))
    def _():
        sources = [reader(got, d) for d in range(4)] + [reader(down, d) for d in range(3)]
        given = {d: powers[d * span : (d + 1) * span, :] for d in range(4)}
        real, imag, _ = make_looks(0, OUTER, sources, weights, given, False, *scratch)
        gamma[:count, :] = real
        gamma[count:, :] = imag

    @pl.when(last)
    def _():
        gamma[...] = jnp.zeros((2 * count, LANES), jnp.float32)


def turn_kernel(got, powers, weights, up_far, gamma, up, sem, *scratch):
    last = is_last()
    span = SPAN[0]

    @pl.when(last)
    def _():
        copy = pltpu.make_async_copy(up_far, up, sem)
        copy.start()
        copy.wait()
        sources = [None, reader(got, 1), reader(got, 2), None, reader(up, 0), reader(up, 1)]
        given = {d: powers[d * span : (d + 1) * span, :] for d in range(4)}
        real, imag, _ = make_looks(0, TURN_BACK, sources, weights, given, False, *scratch)
        gamma[: 2 * span, :] = real
        gamma[2 * span :, :] = imag

    @pl.when(jnp.logical_not(last))
    def _():
        gamma[...] = jnp.zeros((4 * span, LANES), jnp.float32)


def late_kernel(got, weights, gamma, *scratch):
    sources = [reader(got, d) for d in range(4)]
    sources += [reader(got, d, CHUNK[1]) for d in (0, 1, 2, 2, 3)]
    real, imag, _ = make_looks(1, LATE, sources, weights, {}, True, *scratch)
    count = (len(INSIDE) + len(ONWARD)) * SPAN[1]
    gamma[:count, :] = real
    gamma[count:, :] = imag


def gather_kernel(splats, inner, outer, turned, late, out):
    last = is_last()

    def edge(part, number, f):
        if part == 0 and number >= len(INSIDE) + len(ONWARD):
            ref, number, count = turned, number - len(INSIDE) - len(ONWARD), len(TURNED)
        elif part:
            ref, number, count = late, number, len(INSIDE) + len(ONWARD)
        elif number < len(INSIDE):
            ref, count = inner, len(INSIDE)
        else:
            ref, number, count = outer, number - len(INSIDE), len(ONWARD)
        first = (f * count + number) * SPAN[part]
        return ref[first : first + SPAN[part], :]

    for part in range(2):
        back = (6, 7) if part else (12, 13)
        for f in range(2):

            def either_of(usual, other, swap=True):
                there = edge(part, other, f)
                if swap and f:
                    there = -there
                return jnp.where(last, there, edge(part, usual, f))

            table = (
                tuple(edge(part, n, f) for n in (0, 1, 2)),
                (edge(part, 3, f), edge(part, 4, f), either_of(6, back[0], swap=False)),
                (edge(part, 5, f), either_of(7, 1), either_of(8, back[1], swap=False)),
                (either_of(9, 5), either_of(10, 4), either_of(11, 2)),
            )
            for x in range(RING):
                for k in range(3):
                    first = (2 * k + f) * 8 + part * SPAN[0]
                    out[x, first : first + SPAN[part], :] = table[x][k]
    for x in range(RING):
        out[x, 48:56, :] = splats[0:8, :]


def map_kernel(splats, below, own, above, ifg, coh):
    sources = [(ref, q) for ref in (below, own, above) for q in range(4)]
    first = lax.axis_index("band") * 4 + 1
    masks = []
    counts = [jnp.zeros((8, LANES), jnp.float32) for _ in range(4)]
    for ref, q in sources:
        line = ref[q, 48:56, :]
        hit = []
        for m in range(4):
            hit.append(line == (first + m).astype(jnp.float32))
            counts[m] += hit[m].astype(jnp.float32)
        masks.append(hit)
    for pair in range(2):
        offset = splats[8 * pair + 8 : 8 * pair + 16, :]
        near, middle = offset == 1.0, offset == 2.0
        sums = [[jnp.zeros((8, LANES), jnp.float32) for _ in range(4)] for _ in range(3)]
        for (ref, q), hit in zip(sources, masks):

            def chosen(f):
                a, b, c = (ref[q, 16 * k + 8 * f : 16 * k + 8 * f + 8, :] for k in range(3))
                return jnp.where(near, a, jnp.where(middle, b, c))

            real, imag = chosen(0), chosen(1)
            fields = (real, imag, jnp.sqrt(real * real + imag * imag))
            for f in range(3):
                for m in range(4):
                    sums[f][m] += jnp.where(hit[m], fields[f], 0.0)
        for m in range(4):
            divisor = jnp.maximum(counts[m], 1.0)
            for f in range(3):
                value = sums[f][m] / divisor
                for s in range(8):
                    cols = slice(s * LANES, (s + 1) * LANES)
                    if f < 2:
                        ifg[pair, f, m : m + 1, cols] = value[s : s + 1]
                    else:
                        coh[pair, m : m + 1, cols] = value[s : s + 1]


def summing_weights():
    column = np.arange(5 * LANES)
    look = np.arange(LANES) % 32
    table = (column[:, None] // LOOK_C == look[None, :]).astype(np.float32)
    return jnp.asarray(table, jnp.bfloat16)


def passed_along(block, axis, distance):
    devices = range(lax.axis_size(axis))
    route = [(i - distance, i) for i in devices if i - distance in devices]
    return lax.ppermute(block, axis, route)


def moved_layers(block, step, layers=range(LAYERS)):
    route = [
        (RING * z + x, RING * (z + step) + x)
        for z in layers
        for x in range(RING)
        if z + step in range(LAYERS)
    ]
    return lax.ppermute(block, "date", route)


def in_ring(block):
    rings = [[RING * z + x for x in range(RING)] for z in range(LAYERS)]
    return lax.all_to_all(
        block, "date", split_axis=0, concat_axis=0, tiled=True, axis_index_groups=rings
    )


def looks_scratch(part, passes):
    edges, powers, fold = fold_rows(part, passes)
    f32 = jnp.float32
    return [
        pltpu.VMEM((2, edges * ROWS[part], LANES), f32),
        pltpu.VMEM((powers * ROWS[part], LANES), f32),
        pltpu.VMEM((fold, 5 * LANES), f32),
        pltpu.VMEM((edges * SPAN[part], LANES), f32),
    ]


def body(radar_image_cube, orbit_separations, epoch_couple_matrix, averaged_line_grid_lines):
    f32, bf16 = jnp.float32, jnp.bfloat16
    smem = pl.BlockSpec(memory_space=pltpu.SMEM)
    vmem = pl.BlockSpec(memory_space=pltpu.VMEM)
    hbm = pl.BlockSpec(memory_space=pltpu.HBM)

    def table(*shape, dtype=f32):
        return jax.ShapeDtypeStruct(shape, dtype)

    def call(kernel, outs, name, ins, scratch=(), limit=8, scalars=0, flops=0, moved=4_000_000, far=0):
        return pl.pallas_call(
            kernel,
            out_shape=outs,
            in_specs=[smem] * scalars + [vmem] * (len(ins) - scalars - far) + [hbm] * far,
            out_specs=[vmem] * len(outs),
            scratch_shapes=list(scratch),
            compiler_params=pltpu.CompilerParams(vmem_limit_bytes=limit << 20),
            cost_estimate=pl.CostEstimate(
                flops=flops, bytes_accessed=moved, transcendentals=0
            ),
            name=name,
        )(*ins)

    cube = radar_image_cube.reshape(2, 20, 160, LANES)
    cube = cube.transpose(1, 2, 0, 3).reshape(RING, LOOK_R * ALL_ROWS, LANES)
    separation = orbit_separations.reshape(1, 1)
    weights = summing_weights()
    sent, raw = call(
        first_pack,
        (table(RING, CHUNK[0], LANES, dtype=bf16), table(RING, CHUNK[1], LANES, dtype=bf16)),
        "first_pack",
        (cube, separation),
    )
    got = in_ring(sent)
    down = moved_layers(raw, -1)
    up = moved_layers(raw, 1, (LAYERS - 2,))
    both, splats = call(
        second_pack,
        (table(RING, 2 * CHUNK[1], LANES, dtype=bf16), table(24, LANES)),
        "second_pack",
        (averaged_line_grid_lines, epoch_couple_matrix, raw, down, up),
        scalars=2,
    )
    got_late = in_ring(both)
    onward = moved_layers(got[0:3], -1)
    backward = moved_layers(got[2:4], 1, (LAYERS - 2,))
    inner, powers = call(
        inner_kernel,
        (table(12 * SPAN[0], LANES), table(4 * SPAN[0], LANES)),
        "inner_looks",
        (got, weights),
        looks_scratch(0, INNER),
        12,
        flops=10_000_000,
    )
    (turned,) = call(
        turn_kernel,
        (table(4 * SPAN[0], LANES),),
        "turned_looks",
        (got, powers, weights, backward),
        [pltpu.VMEM((2, CHUNK[0], LANES), bf16), pltpu.SemaphoreType.DMA]
        + looks_scratch(0, TURN_BACK),
        12,
        flops=10000000,
        moved=4000000,
        far=1,
    )
    (outer,) = call(
        outer_kernel,
        (table(12 * SPAN[0], LANES),),
        "outer_looks",
        (got, onward, powers, weights),
        looks_scratch(0, OUTER),
        12,
        flops=10_000_000,
    )
    (late,) = call(
        late_kernel,
        (table(24 * SPAN[1], LANES),),
        "late_looks",
        (got_late, weights),
        looks_scratch(1, LATE),
        12,
        flops=10_000_000,
    )
    (by_owner,) = call(
        gather_kernel,
        (table(RING, 56, LANES),),
        "by_owner",
        (splats, inner, outer, turned, late),
        limit=4,
    )
    own = in_ring(by_owner)
    below = passed_along(own, "band", 1)
    above = passed_along(own, "band", -1)
    return tuple(
        call(
            map_kernel,
            (table(2, 2, 4, 1024), table(2, 4, 1024)),
            "map_rows",
            (splats, below, own, above),
            limit=4,
        )
    )


def solution(mesh):
    placed = (P("date", None, "band", None), P("date"), P("date", None), P("band"))
    return jax.shard_map(
        body,
        mesh=mesh,
        in_specs=placed,
        out_specs=(P("date", None, "band", None), P("date", "band", None)),
        check_vma=False,
    )
```

```python
import math

import jax
import jax.numpy as jnp
import numpy as np
from jax import lax
from jax.experimental import pallas as pl
from jax.experimental.pallas import tpu as pltpu
from jax.sharding import PartitionSpec as P

LOOK_R = 5
LOOK_C = 20
LANES = 128
RING = 4
LAYERS = 8
TURN = 2.0 * math.pi
TILES = (120, 40)
FIRST = (0, TILES[0])
USED = tuple(2 * tiles for tiles in TILES)
ROWS = tuple((used + 15) // 16 * 16 for used in USED)
DATA = tuple(LOOK_R * rows for rows in ROWS)
CHUNK = tuple(data + 16 for data in DATA)
GROUPS = tuple(tiles // 5 for tiles in TILES)
SPAN = tuple(groups // 4 for groups in GROUPS)
ALL_ROWS = sum(USED)
INSIDE = ((0, 1), (0, 2), (0, 3), (1, 2), (1, 3), (2, 3))
ONWARD = ((1, 4), (2, 4), (2, 5), (3, 4), (3, 5), (3, 6))
TURNED = ((1, 4), (2, 5))
BACKWARD = (((1, 7), (1, 4)), ((2, 8), (2, 4)))
INSTEAD = {7: 4, 8: 5}


def is_last():
    return lax.axis_index("date") // RING == LAYERS - 1


def two_parts(value):
    high = value.astype(jnp.bfloat16)
    low = (value - high.astype(jnp.float32)).astype(jnp.bfloat16)
    return high, low


def first_pack(cube, separation, out, raw):
    value = separation[...].astype(jnp.float32)
    tail = jnp.broadcast_to(value, (16, LANES)).astype(jnp.bfloat16)
    for part, ref in enumerate((out, raw)):
        for q in range(RING):
            ref[q, DATA[part] : CHUNK[part], :] = tail
            for r in range(LOOK_R):
                first = r * ALL_ROWS + 2 * FIRST[part]
                block = cube[q, first : first + USED[part], :]
                if ROWS[part] > USED[part]:
                    more = jnp.zeros((ROWS[part] - USED[part], LANES), jnp.bfloat16)
                    block = jnp.concatenate([block, more])
                ref[q, r * ROWS[part] : (r + 1) * ROWS[part], :] = block


def second_pack(lines, couples, raw, down, up, out, splats):
    out[:, : CHUNK[1], :] = raw[...]
    last = is_last()

    @pl.when(last)
    def _():
        out[:, CHUNK[1] :, :] = up[...]

    @pl.when(jnp.logical_not(last))
    def _():
        out[:, CHUNK[1] :, :] = down[...]

    line = lines[lax.axis_index("date") % RING] + 1
    splats[0:8, :] = jnp.full((8, LANES), line, jnp.int32).astype(jnp.float32)
    for pair in range(2):
        offset = jnp.abs(couples[pair, 1] - couples[pair, 0])
        here = slice(8 * pair + 8, 8 * pair + 16)
        splats[here, :] = jnp.full((8, LANES), offset, jnp.int32).astype(jnp.float32)


def fold_rows(part, passes):
    edges = sum(len(edges) for edges, _ in passes)
    powers = sum(len(powers) for _, powers in passes)
    rows = (2 * edges + powers) * GROUPS[part]
    return edges, powers, (rows + 15) // 16 * 16


def make_looks(part, passes, sources, weights, given, swap, cross, power, terms, norm):
    rows_of, groups, span = ROWS[part], GROUPS[part], SPAN[part]
    edges = [e for step in passes for e in step[0]]
    dates = [d for step in passes for d in step[1]]
    _, _, fold = fold_rows(part, passes)
    parity = lax.broadcasted_iota(jnp.int32, (8, LANES), 0) % 2 == 0

    def turned(block):
        return jnp.where(parity, -pltpu.roll(block, 7, 0), pltpu.roll(block, 1, 0))

    def products(some, powers, edge_place, power_place):
        partners = sorted({b for _, b in some})
        used = sorted({d for e in some for d in e} | set(powers))

        def step(v, _):
            sums_a = [[None, None] for _ in some]
            sums_b = [[None, None] for _ in some]
            squares = {d: [None, None] for d in powers}
            for r in range(LOOK_R):
                wide = {d: sources[d](r * rows_of + v * 16, 16) for d in used}
                for half in range(2):
                    cut = {d: wide[d][8 * half : 8 * half + 8] for d in used}
                    turn = {d: turned(cut[d]) for d in partners}
                    for i, (a, b) in enumerate(some):
                        add_a, add_b = cut[a] * cut[b], cut[a] * turn[b]
                        sums_a[i][half] = add_a if r == 0 else sums_a[i][half] + add_a
                        sums_b[i][half] = add_b if r == 0 else sums_b[i][half] + add_b
                    for d in powers:
                        square = cut[d] * cut[d]
                        squares[d][half] = square if r == 0 else squares[d][half] + square
            for half in range(2):
                for i in range(len(some)):
                    place = edge_place[i] * rows_of + 8 * half
                    here = pl.ds(pl.multiple_of(place + v * 16, 8), 8)
                    cross[0, here, :] = sums_a[i][half]
                    cross[1, here, :] = sums_b[i][half]
                for i, d in enumerate(powers):
                    place = power_place[i] * rows_of + 8 * half
                    here = pl.ds(pl.multiple_of(place + v * 16, 8), 8)
                    power[here, :] = squares[d][half]
            return 0

        lax.fori_loop(0, rows_of // 16, step, 0)

    def run(some, powers):
        products(some, powers, [edges.index(e) for e in some], [dates.index(d) for d in powers])

    last = is_last()
    for some, powers in passes:
        if not swap or some != ONWARD:
            run(some, powers)
            continue

        @pl.when(jnp.logical_not(last))
        def _():
            run(some, powers)

        @pl.when(last)
        def _():
            wanted = [e for _, e in BACKWARD]
            products(
                [e for e, _ in BACKWARD],
                list(INSTEAD),
                [edges.index(e) for e in wanted],
                [dates.index(d) for d in INSTEAD.values()],
            )
            nothing = jnp.zeros((rows_of, LANES), jnp.float32)
            for e in some:
                if e not in wanted:
                    here = slice(edges.index(e) * rows_of, (edges.index(e) + 1) * rows_of)
                    cross[0, here, :] = nothing
                    cross[1, here, :] = nothing
            for d in powers:
                if d not in INSTEAD.values():
                    power[dates.index(d) * rows_of : (dates.index(d) + 1) * rows_of, :] = nothing

    group = lax.broadcasted_iota(jnp.int32, (groups, LANES), 0)
    lane = lax.broadcasted_iota(jnp.int32, (groups, LANES), 1)
    tile = (FIRST[part] + 5 * group).astype(jnp.float32)
    within = lane.astype(jnp.float32) * (1.0 / LANES)
    field = len(edges) * groups
    repeats = (groups + 7) // 8

    def keep(place, k, value):
        terms[place : place + groups, k * LANES : (k + 1) * LANES] = value

    base = [read and read(DATA[part], 16)[:8] for read in sources]
    instead = {e: d for (_, d), e in BACKWARD} if swap else {}
    for i, (a, b) in enumerate(edges):
        other = base[b]
        if (a, b) in instead:
            other = jnp.where(last, base[instead[a, b]], other)
        delta = base[a] - other
        once = (delta - jnp.round(delta)) * TURN
        turn_c = jnp.concatenate([jnp.cos(once)] * repeats)[:groups]
        turn_s = jnp.concatenate([jnp.sin(once)] * repeats)[:groups]
        delta = jnp.concatenate([delta] * repeats)[:groups]
        turns = delta * tile
        turns = (turns - jnp.round(turns)) + delta * within
        angle = (turns - jnp.round(turns)) * TURN
        cosine, sine = jnp.cos(angle), jnp.sin(angle)
        for k in range(5):
            even = pl.ds(i * rows_of + 2 * k, groups, stride=10)
            odd = pl.ds(i * rows_of + 2 * k + 1, groups, stride=10)
            prod_r = cross[0, even, :] + cross[0, odd, :]
            prod_i = cross[1, even, :] + cross[1, odd, :]
            keep(i * groups, k, prod_r * cosine + prod_i * sine)
            keep(field + i * groups, k, prod_i * cosine - prod_r * sine)
            if k < 4:
                cosine, sine = cosine * turn_c - sine * turn_s, sine * turn_c + cosine * turn_s
    for d in range(len(dates)):
        for k in range(5):
            even = pl.ds(d * rows_of + 2 * k, groups, stride=10)
            odd = pl.ds(d * rows_of + 2 * k + 1, groups, stride=10)
            keep(2 * field + d * groups, k, power[even, :] + power[odd, :])
    filled = 2 * field + len(dates) * groups
    if fold > filled:
        terms[filled:fold, :] = jnp.zeros((fold - filled, 5 * LANES), jnp.float32)

    high, low = two_parts(terms[...])
    summed = jnp.dot(high, weights[...], preferred_element_type=jnp.float32)
    summed += jnp.dot(low, weights[...], preferred_element_type=jnp.float32)
    row = lax.broadcasted_iota(jnp.int32, (fold, LANES), 0)
    lane = lax.broadcasted_iota(jnp.int32, (fold, LANES), 1)
    high, low = two_parts(jnp.where(lane // 32 == row % 4, summed, 0.0))
    joined = (
        lax.broadcasted_iota(jnp.int32, (fold // 4, fold), 0)
        == lax.broadcasted_iota(jnp.int32, (fold // 4, fold), 1) // 4
    ).astype(jnp.bfloat16)
    looks = jnp.dot(joined, high, preferred_element_type=jnp.float32) + jnp.dot(
        joined, low, preferred_element_type=jnp.float32
    )
    looks = looks * (1.0 / (LOOK_R * LOOK_C))
    count = len(edges) * span
    means = dict(given)
    for i, d in enumerate(dates):
        first = 2 * count + i * span
        means[d] = looks[first : first + span]
    for i, (a, b) in enumerate(edges):
        other = means[b]
        if (a, b) in instead:
            other = jnp.where(last, means[INSTEAD[instead[a, b]]], other)
        norm[i * span : (i + 1) * span, :] = means[a] * other
    inverse = 1.0 / jnp.sqrt(norm[...] + 1e-06)
    return looks[:count] * inverse, looks[count : 2 * count] * inverse, means


INNER = ((INSIDE, (0, 1, 2, 3)),)
OUTER = ((ONWARD, (4, 5, 6)),)
TURN_BACK = ((TURNED, (4, 5)),)
LATE = ((INSIDE, (0, 1, 2, 3)), (ONWARD, (4, 5, 6)))


def reader(ref, date, offset=0):
    def read(first, count):
        start = first + offset
        if not isinstance(start, int):
            start = pl.multiple_of(start, 16)
        return ref[date, pl.ds(start, count), :].astype(jnp.float32)

    return read


def inner_kernel(got, weights, gamma, powers, *scratch):
    sources = [reader(got, d) for d in range(4)]
    real, imag, means = make_looks(0, INNER, sources, weights, {}, False, *scratch)
    count = len(INSIDE) * SPAN[0]
    gamma[:count, :] = real
    gamma[count:, :] = imag
    for d in range(4):
        powers[d * SPAN[0] : (d + 1) * SPAN[0], :] = means[d]


def outer_kernel(got, down, powers, weights, gamma, *scratch):
    last = is_last()
    span = SPAN[0]
    count = len(ONWARD) * span

    @pl.when(jnp.logical_not(last))
    def _():
        sources = [reader(got, d) for d in range(4)] + [reader(down, d) for d in range(3)]
        given = {d: powers[d * span : (d + 1) * span, :] for d in range(4)}
        real, imag, _ = make_looks(0, OUTER, sources, weights, given, False, *scratch)
        gamma[:count, :] = real
        gamma[count:, :] = imag

    @pl.when(last)
    def _():
        gamma[...] = jnp.zeros((2 * count, LANES), jnp.float32)


def turn_kernel(got, powers, weights, up_far, gamma, up, sem, *scratch):
    last = is_last()
    span = SPAN[0]

    @pl.when(last)
    def _():
        copy = pltpu.make_async_copy(up_far, up, sem)
        copy.start()
        copy.wait()
        sources = [None, reader(got, 1), reader(got, 2), None, reader(up, 1), reader(up, 2)]
        given = {d: powers[d * span : (d + 1) * span, :] for d in range(4)}
        real, imag, _ = make_looks(0, TURN_BACK, sources, weights, given, False, *scratch)
        gamma[: 2 * span, :] = real
        gamma[2 * span :, :] = imag

    @pl.when(jnp.logical_not(last))
    def _():
        gamma[...] = jnp.zeros((4 * span, LANES), jnp.float32)


def late_kernel(got, weights, gamma, *scratch):
    sources = [reader(got, d) for d in range(4)]
    sources += [reader(got, d, CHUNK[1]) for d in (0, 1, 2, 2, 3)]
    real, imag, _ = make_looks(1, LATE, sources, weights, {}, True, *scratch)
    count = (len(INSIDE) + len(ONWARD)) * SPAN[1]
    gamma[:count, :] = real
    gamma[count:, :] = imag


def gather_kernel(splats, inner, outer, turned, late, out):
    last = is_last()

    def edge(part, number, f):
        if part == 0 and number >= len(INSIDE) + len(ONWARD):
            ref, number, count = turned, number - len(INSIDE) - len(ONWARD), len(TURNED)
        elif part:
            ref, number, count = late, number, len(INSIDE) + len(ONWARD)
        elif number < len(INSIDE):
            ref, count = inner, len(INSIDE)
        else:
            ref, number, count = outer, number - len(INSIDE), len(ONWARD)
        first = (f * count + number) * SPAN[part]
        return ref[first : first + SPAN[part], :]

    for part in range(2):
        back = (6, 7) if part else (12, 13)
        for f in range(2):

            def either_of(usual, other, swap=True):
                there = edge(part, other, f)
                if swap and f:
                    there = -there
                return jnp.where(last, there, edge(part, usual, f))

            table = (
                tuple(edge(part, n, f) for n in (0, 1, 2)),
                (edge(part, 3, f), edge(part, 4, f), either_of(6, back[0], swap=False)),
                (edge(part, 5, f), either_of(7, 1), either_of(8, back[1], swap=False)),
                (either_of(9, 5), either_of(10, 4), either_of(11, 2)),
            )
            for x in range(RING):
                for k in range(3):
                    first = (2 * k + f) * 8 + part * SPAN[0]
                    out[x, first : first + SPAN[part], :] = table[x][k]
    for x in range(RING):
        out[x, 48:56, :] = splats[0:8, :]


def map_kernel(splats, below, own, above, ifg, coh):
    sources = [(ref, q) for ref in (below, own, above) for q in range(4)]
    first = lax.axis_index("band") * 4 + 1
    masks = []
    counts = [jnp.zeros((8, LANES), jnp.float32) for _ in range(4)]
    for ref, q in sources:
        line = ref[q, 48:56, :]
        hit = []
        for m in range(4):
            hit.append(line == (first + m).astype(jnp.float32))
            counts[m] += hit[m].astype(jnp.float32)
        masks.append(hit)
    for pair in range(2):
        offset = splats[8 * pair + 8 : 8 * pair + 16, :]
        near, middle = offset == 1.0, offset == 2.0
        sums = [[jnp.zeros((8, LANES), jnp.float32) for _ in range(4)] for _ in range(3)]
        for (ref, q), hit in zip(sources, masks):

            def chosen(f):
                a, b, c = (ref[q, 16 * k + 8 * f : 16 * k + 8 * f + 8, :] for k in range(3))
                return jnp.where(near, a, jnp.where(middle, b, c))

            real, imag = chosen(0), chosen(1)
            fields = (real, imag, jnp.sqrt(real * real + imag * imag))
            for f in range(3):
                for m in range(4):
                    sums[f][m] += jnp.where(hit[m], fields[f], 0.0)
        for m in range(4):
            divisor = jnp.maximum(counts[m], 1.0)
            for f in range(3):
                value = sums[f][m] / divisor
                for s in range(8):
                    cols = slice(s * LANES, (s + 1) * LANES)
                    if f < 2:
                        ifg[pair, f, m : m + 1, cols] = value[s : s + 1]
                    else:
                        coh[pair, m : m + 1, cols] = value[s : s + 1]


def summing_weights():
    column = np.arange(5 * LANES)
    look = np.arange(LANES) % 32
    table = (column[:, None] // LOOK_C == look[None, :]).astype(np.float32)
    return jnp.asarray(table, jnp.bfloat16)


def passed_along(block, axis, distance):
    devices = range(lax.axis_size(axis))
    route = [(i - distance, i) for i in devices if i - distance in devices]
    return lax.ppermute(block, axis, route)


def moved_layers(block, step, layers=range(LAYERS)):
    route = [
        (RING * z + x, RING * (z + step) + x)
        for z in layers
        for x in range(RING)
        if z + step in range(LAYERS)
    ]
    return lax.ppermute(block, "date", route)


def in_ring(block):
    rings = [[RING * z + x for x in range(RING)] for z in range(LAYERS)]
    return lax.all_to_all(
        block, "date", split_axis=0, concat_axis=0, tiled=True, axis_index_groups=rings
    )


def looks_scratch(part, passes):
    edges, powers, fold = fold_rows(part, passes)
    f32 = jnp.float32
    return [
        pltpu.VMEM((2, edges * ROWS[part], LANES), f32),
        pltpu.VMEM((powers * ROWS[part], LANES), f32),
        pltpu.VMEM((fold, 5 * LANES), f32),
        pltpu.VMEM((edges * SPAN[part], LANES), f32),
    ]


def body(radar_image_cube, orbit_separations, epoch_couple_matrix, averaged_line_grid_lines):
    f32, bf16 = jnp.float32, jnp.bfloat16
    smem = pl.BlockSpec(memory_space=pltpu.SMEM)
    vmem = pl.BlockSpec(memory_space=pltpu.VMEM)
    hbm = pl.BlockSpec(memory_space=pltpu.HBM)

    def table(*shape, dtype=f32):
        return jax.ShapeDtypeStruct(shape, dtype)

    def call(kernel, outs, name, ins, scratch=(), limit=8, scalars=0, flops=0, moved=4_000_000, far=0):
        return pl.pallas_call(
            kernel,
            out_shape=outs,
            in_specs=[smem] * scalars + [vmem] * (len(ins) - scalars - far) + [hbm] * far,
            out_specs=[vmem] * len(outs),
            scratch_shapes=list(scratch),
            compiler_params=pltpu.CompilerParams(vmem_limit_bytes=limit << 20),
            cost_estimate=pl.CostEstimate(
                flops=flops, bytes_accessed=moved, transcendentals=0
            ),
            name=name,
        )(*ins)

    cube = radar_image_cube.reshape(2, 20, 160, LANES)
    cube = cube.transpose(1, 2, 0, 3).reshape(RING, LOOK_R * ALL_ROWS, LANES)
    separation = orbit_separations.reshape(1, 1)
    weights = summing_weights()
    sent, raw = call(
        first_pack,
        (table(RING, CHUNK[0], LANES, dtype=bf16), table(RING, CHUNK[1], LANES, dtype=bf16)),
        "first_pack",
        (cube, separation),
    )
    got = in_ring(sent)
    down = moved_layers(raw, -1)
    up = moved_layers(raw, 1, (LAYERS - 2,))
    both, splats = call(
        second_pack,
        (table(RING, 2 * CHUNK[1], LANES, dtype=bf16), table(24, LANES)),
        "second_pack",
        (averaged_line_grid_lines, epoch_couple_matrix, raw, down, up),
        scalars=2,
    )
    got_late = in_ring(both)
    onward = moved_layers(got[0:3], -1)
    backward = moved_layers(got[1:4], 1, (LAYERS - 2,))
    inner, powers = call(
        inner_kernel,
        (table(12 * SPAN[0], LANES), table(4 * SPAN[0], LANES)),
        "inner_looks",
        (got, weights),
        looks_scratch(0, INNER),
        12,
        flops=10_000_000,
    )
    (turned,) = call(
        turn_kernel,
        (table(4 * SPAN[0], LANES),),
        "turned_looks",
        (got, powers, weights, backward),
        [pltpu.VMEM((3, CHUNK[0], LANES), bf16), pltpu.SemaphoreType.DMA]
        + looks_scratch(0, TURN_BACK),
        12,
        flops=10000000,
        moved=4000000,
        far=1,
    )
    (outer,) = call(
        outer_kernel,
        (table(12 * SPAN[0], LANES),),
        "outer_looks",
        (got, onward, powers, weights),
        looks_scratch(0, OUTER),
        12,
        flops=10_000_000,
    )
    (late,) = call(
        late_kernel,
        (table(24 * SPAN[1], LANES),),
        "late_looks",
        (got_late, weights),
        looks_scratch(1, LATE),
        12,
        flops=10_000_000,
    )
    (by_owner,) = call(
        gather_kernel,
        (table(RING, 56, LANES),),
        "by_owner",
        (splats, inner, outer, turned, late),
        limit=4,
    )
    own = in_ring(by_owner)
    below = passed_along(own, "band", 1)
    above = passed_along(own, "band", -1)
    return tuple(
        call(
            map_kernel,
            (table(2, 2, 4, 1024), table(2, 4, 1024)),
            "map_rows",
            (splats, below, own, above),
            limit=4,
        )
    )


def solution(mesh):
    placed = (P("date", None, "band", None), P("date"), P("date", None), P("band"))
    return jax.shard_map(
        body,
        mesh=mesh,
        in_specs=placed,
        out_specs=(P("date", None, "band", None), P("date", "band", None)),
        check_vma=False,
    )
```

```python
import math

import jax
import jax.numpy as jnp
import numpy as np
from jax import lax
from jax.experimental import pallas as pl
from jax.experimental.pallas import tpu as pltpu
from jax.sharding import PartitionSpec as P

LOOK_R = 5
LOOK_C = 20
LANES = 128
RING = 4
LAYERS = 8
TURN = 2.0 * math.pi
TILES = (120, 40)
FIRST = (0, TILES[0])
USED = tuple(2 * tiles for tiles in TILES)
ROWS = tuple((used + 15) // 16 * 16 for used in USED)
DATA = tuple(LOOK_R * rows for rows in ROWS)
CHUNK = tuple(data + 16 for data in DATA)
GROUPS = tuple(tiles // 5 for tiles in TILES)
SPAN = tuple(groups // 4 for groups in GROUPS)
ALL_ROWS = sum(USED)
INSIDE = ((0, 1), (0, 2), (0, 3), (1, 2), (1, 3), (2, 3))
ONWARD = ((1, 4), (2, 4), (2, 5), (3, 4), (3, 5), (3, 6))
TURNED = ((1, 4), (2, 5))
BACKWARD = (((1, 7), (1, 4)), ((2, 8), (2, 4)))
INSTEAD = {7: 4, 8: 5}


def is_last():
    return lax.axis_index("date") // RING == LAYERS - 1


def two_parts(value):
    high = value.astype(jnp.bfloat16)
    low = (value - high.astype(jnp.float32)).astype(jnp.bfloat16)
    return high, low


def first_pack(cube, separation, out, raw):
    value = separation[...].astype(jnp.float32)
    tail = jnp.broadcast_to(value, (16, LANES)).astype(jnp.bfloat16)
    for part, ref in enumerate((out, raw)):
        for q in range(RING):
            ref[q, DATA[part] : CHUNK[part], :] = tail
            for r in range(LOOK_R):
                first = r * ALL_ROWS + 2 * FIRST[part]
                block = cube[q, first : first + USED[part], :]
                if ROWS[part] > USED[part]:
                    more = jnp.zeros((ROWS[part] - USED[part], LANES), jnp.bfloat16)
                    block = jnp.concatenate([block, more])
                ref[q, r * ROWS[part] : (r + 1) * ROWS[part], :] = block


def second_pack(lines, couples, raw, down, up, out, splats):
    out[:, : CHUNK[1], :] = raw[...]
    last = is_last()

    @pl.when(last)
    def _():
        out[:, CHUNK[1] :, :] = up[...]

    @pl.when(jnp.logical_not(last))
    def _():
        out[:, CHUNK[1] :, :] = down[...]

    line = lines[lax.axis_index("date") % RING] + 1
    splats[0:8, :] = jnp.full((8, LANES), line, jnp.int32).astype(jnp.float32)
    for pair in range(2):
        offset = jnp.abs(couples[pair, 1] - couples[pair, 0])
        here = slice(8 * pair + 8, 8 * pair + 16)
        splats[here, :] = jnp.full((8, LANES), offset, jnp.int32).astype(jnp.float32)


def fold_rows(part, passes):
    edges = sum(len(edges) for edges, _ in passes)
    powers = sum(len(powers) for _, powers in passes)
    rows = (2 * edges + powers) * GROUPS[part]
    return edges, powers, (rows + 15) // 16 * 16


def make_looks(part, passes, sources, weights, given, swap, cross, power, terms, norm):
    rows_of, groups, span = ROWS[part], GROUPS[part], SPAN[part]
    edges = [e for step in passes for e in step[0]]
    dates = [d for step in passes for d in step[1]]
    _, _, fold = fold_rows(part, passes)
    parity = lax.broadcasted_iota(jnp.int32, (8, LANES), 0) % 2 == 0

    def turned(block):
        return jnp.where(parity, -pltpu.roll(block, 7, 0), pltpu.roll(block, 1, 0))

    def products(some, powers, edge_place, power_place):
        partners = sorted({b for _, b in some})
        used = sorted({d for e in some for d in e} | set(powers))

        def step(v, _):
            sums_a = [[None, None] for _ in some]
            sums_b = [[None, None] for _ in some]
            squares = {d: [None, None] for d in powers}
            for r in range(LOOK_R):
                wide = {d: sources[d](r * rows_of + v * 16, 16) for d in used}
                for half in range(2):
                    cut = {d: wide[d][8 * half : 8 * half + 8] for d in used}
                    turn = {d: turned(cut[d]) for d in partners}
                    for i, (a, b) in enumerate(some):
                        add_a, add_b = cut[a] * cut[b], cut[a] * turn[b]
                        sums_a[i][half] = add_a if r == 0 else sums_a[i][half] + add_a
                        sums_b[i][half] = add_b if r == 0 else sums_b[i][half] + add_b
                    for d in powers:
                        square = cut[d] * cut[d]
                        squares[d][half] = square if r == 0 else squares[d][half] + square
            for half in range(2):
                for i in range(len(some)):
                    place = edge_place[i] * rows_of + 8 * half
                    here = pl.ds(pl.multiple_of(place + v * 16, 8), 8)
                    cross[0, here, :] = sums_a[i][half]
                    cross[1, here, :] = sums_b[i][half]
                for i, d in enumerate(powers):
                    place = power_place[i] * rows_of + 8 * half
                    here = pl.ds(pl.multiple_of(place + v * 16, 8), 8)
                    power[here, :] = squares[d][half]
            return 0

        lax.fori_loop(0, rows_of // 16, step, 0)

    def run(some, powers):
        products(some, powers, [edges.index(e) for e in some], [dates.index(d) for d in powers])

    last = is_last()
    for some, powers in passes:
        if not swap or some != ONWARD:
            run(some, powers)
            continue

        @pl.when(jnp.logical_not(last))
        def _():
            run(some, powers)

        @pl.when(last)
        def _():
            wanted = [e for _, e in BACKWARD]
            products(
                [e for e, _ in BACKWARD],
                list(INSTEAD),
                [edges.index(e) for e in wanted],
                [dates.index(d) for d in INSTEAD.values()],
            )
            nothing = jnp.zeros((rows_of, LANES), jnp.float32)
            for e in some:
                if e not in wanted:
                    here = slice(edges.index(e) * rows_of, (edges.index(e) + 1) * rows_of)
                    cross[0, here, :] = nothing
                    cross[1, here, :] = nothing
            for d in powers:
                if d not in INSTEAD.values():
                    power[dates.index(d) * rows_of : (dates.index(d) + 1) * rows_of, :] = nothing

    group = lax.broadcasted_iota(jnp.int32, (groups, LANES), 0)
    lane = lax.broadcasted_iota(jnp.int32, (groups, LANES), 1)
    tile = (FIRST[part] + 5 * group).astype(jnp.float32)
    within = lane.astype(jnp.float32) * (1.0 / LANES)
    field = len(edges) * groups
    repeats = (groups + 7) // 8

    def keep(place, k, value):
        terms[place : place + groups, k * LANES : (k + 1) * LANES] = value

    base = [read and read(DATA[part], 16)[:8] for read in sources]
    instead = {e: d for (_, d), e in BACKWARD} if swap else {}
    for i, (a, b) in enumerate(edges):
        other = base[b]
        if (a, b) in instead:
            other = jnp.where(last, base[instead[a, b]], other)
        delta = base[a] - other
        once = (delta - jnp.round(delta)) * TURN
        turn_c = jnp.concatenate([jnp.cos(once)] * repeats)[:groups]
        turn_s = jnp.concatenate([jnp.sin(once)] * repeats)[:groups]
        delta = jnp.concatenate([delta] * repeats)[:groups]
        turns = delta * tile
        turns = (turns - jnp.round(turns)) + delta * within
        angle = (turns - jnp.round(turns)) * TURN
        cosine, sine = jnp.cos(angle), jnp.sin(angle)
        for k in range(5):
            even = pl.ds(i * rows_of + 2 * k, groups, stride=10)
            odd = pl.ds(i * rows_of + 2 * k + 1, groups, stride=10)
            prod_r = cross[0, even, :] + cross[0, odd, :]
            prod_i = cross[1, even, :] + cross[1, odd, :]
            keep(i * groups, k, prod_r * cosine + prod_i * sine)
            keep(field + i * groups, k, prod_i * cosine - prod_r * sine)
            if k < 4:
                cosine, sine = cosine * turn_c - sine * turn_s, sine * turn_c + cosine * turn_s
    for d in range(len(dates)):
        for k in range(5):
            even = pl.ds(d * rows_of + 2 * k, groups, stride=10)
            odd = pl.ds(d * rows_of + 2 * k + 1, groups, stride=10)
            keep(2 * field + d * groups, k, power[even, :] + power[odd, :])
    filled = 2 * field + len(dates) * groups
    if fold > filled:
        terms[filled:fold, :] = jnp.zeros((fold - filled, 5 * LANES), jnp.float32)

    high, low = two_parts(terms[...])
    summed = jnp.dot(high, weights[...], preferred_element_type=jnp.float32)
    summed += jnp.dot(low, weights[...], preferred_element_type=jnp.float32)
    row = lax.broadcasted_iota(jnp.int32, (fold, LANES), 0)
    lane = lax.broadcasted_iota(jnp.int32, (fold, LANES), 1)
    high, low = two_parts(jnp.where(lane // 32 == row % 4, summed, 0.0))
    joined = (
        lax.broadcasted_iota(jnp.int32, (fold // 4, fold), 0)
        == lax.broadcasted_iota(jnp.int32, (fold // 4, fold), 1) // 4
    ).astype(jnp.bfloat16)
    looks = jnp.dot(joined, high, preferred_element_type=jnp.float32) + jnp.dot(
        joined, low, preferred_element_type=jnp.float32
    )
    looks = looks * (1.0 / (LOOK_R * LOOK_C))
    count = len(edges) * span
    means = dict(given)
    for i, d in enumerate(dates):
        first = 2 * count + i * span
        means[d] = looks[first : first + span]
    for i, (a, b) in enumerate(edges):
        other = means[b]
        if (a, b) in instead:
            other = jnp.where(last, means[INSTEAD[instead[a, b]]], other)
        norm[i * span : (i + 1) * span, :] = means[a] * other
    inverse = 1.0 / jnp.sqrt(norm[...] + 1e-06)
    return looks[:count] * inverse, looks[count : 2 * count] * inverse, means


INNER = ((INSIDE, (0, 1, 2, 3)),)
OUTER = ((ONWARD, (4, 5, 6)),)
TURN_BACK = ((TURNED, (4, 5)),)
LATE = ((INSIDE, (0, 1, 2, 3)), (ONWARD, (4, 5, 6)))


def reader(ref, date, offset=0):
    def read(first, count):
        start = first + offset
        if not isinstance(start, int):
            start = pl.multiple_of(start, 16)
        return ref[date, pl.ds(start, count), :].astype(jnp.float32)

    return read


def inner_kernel(got, weights, gamma, powers, *scratch):
    sources = [reader(got, d) for d in range(4)]
    real, imag, means = make_looks(0, INNER, sources, weights, {}, False, *scratch)
    count = len(INSIDE) * SPAN[0]
    gamma[:count, :] = real
    gamma[count:, :] = imag
    for d in range(4):
        powers[d * SPAN[0] : (d + 1) * SPAN[0], :] = means[d]


def outer_kernel(got, down, powers, weights, gamma, *scratch):
    last = is_last()
    span = SPAN[0]
    count = len(ONWARD) * span

    @pl.when(jnp.logical_not(last))
    def _():
        sources = [reader(got, d) for d in range(4)] + [reader(down, d) for d in range(3)]
        given = {d: powers[d * span : (d + 1) * span, :] for d in range(4)}
        real, imag, _ = make_looks(0, OUTER, sources, weights, given, False, *scratch)
        gamma[:count, :] = real
        gamma[count:, :] = imag

    @pl.when(last)
    def _():
        gamma[...] = jnp.zeros((2 * count, LANES), jnp.float32)


def turn_kernel(got, powers, weights, up_far, gamma, up, sem, *scratch):
    last = is_last()
    span = SPAN[0]

    @pl.when(last)
    def _():
        copy = pltpu.make_async_copy(up_far, up, sem)
        copy.start()
        copy.wait()
        sources = [None, reader(got, 1), reader(got, 2), None, reader(up, 1), reader(up, 2)]
        given = {d: powers[d * span : (d + 1) * span, :] for d in range(4)}
        real, imag, _ = make_looks(0, TURN_BACK, sources, weights, given, False, *scratch)
        gamma[: 2 * span, :] = real
        gamma[2 * span :, :] = imag

    @pl.when(jnp.logical_not(last))
    def _():
        gamma[...] = jnp.zeros((4 * span, LANES), jnp.float32)


def late_kernel(got, weights, gamma, *scratch):
    sources = [reader(got, d) for d in range(4)]
    sources += [reader(got, d, CHUNK[1]) for d in (0, 1, 2, 2, 3)]
    real, imag, _ = make_looks(1, LATE, sources, weights, {}, True, *scratch)
    count = (len(INSIDE) + len(ONWARD)) * SPAN[1]
    gamma[:count, :] = real
    gamma[count:, :] = imag


def gather_kernel(splats, inner, outer, turned, late, out):
    last = is_last()

    def edge(part, number, f):
        if part == 0 and number >= len(INSIDE) + len(ONWARD):
            ref, number, count = turned, number - len(INSIDE) - len(ONWARD), len(TURNED)
        elif part:
            ref, number, count = late, number, len(INSIDE) + len(ONWARD)
        elif number < len(INSIDE):
            ref, count = inner, len(INSIDE)
        else:
            ref, number, count = outer, number - len(INSIDE), len(ONWARD)
        first = (f * count + number) * SPAN[part]
        return ref[first : first + SPAN[part], :]

    for part in range(2):
        back = (6, 7) if part else (12, 13)
        for f in range(2):

            def either_of(usual, other, swap=True):
                there = edge(part, other, f)
                if swap and f:
                    there = -there
                return jnp.where(last, there, edge(part, usual, f))

            table = (
                tuple(edge(part, n, f) for n in (0, 1, 2)),
                (edge(part, 3, f), edge(part, 4, f), either_of(6, back[0], swap=False)),
                (edge(part, 5, f), either_of(7, 1), either_of(8, back[1], swap=False)),
                (either_of(9, 5), either_of(10, 4), either_of(11, 2)),
            )
            for x in range(RING):
                for k in range(3):
                    first = (2 * k + f) * 8 + part * SPAN[0]
                    out[x, first : first + SPAN[part], :] = table[x][k]
    for x in range(RING):
        out[x, 48:56, :] = splats[0:8, :]


def map_kernel(splats, below, own, above, ifg, coh):
    sources = [(ref, q) for ref in (below, own, above) for q in range(4)]
    first = lax.axis_index("band") * 4 + 1
    masks = []
    counts = [jnp.zeros((8, LANES), jnp.float32) for _ in range(4)]
    for ref, q in sources:
        line = ref[q, 48:56, :]
        hit = []
        for m in range(4):
            hit.append(line == (first + m).astype(jnp.float32))
            counts[m] += hit[m].astype(jnp.float32)
        masks.append(hit)
    for pair in range(2):
        offset = splats[8 * pair + 8 : 8 * pair + 16, :]
        near, middle = offset == 1.0, offset == 2.0
        sums = [[jnp.zeros((8, LANES), jnp.float32) for _ in range(4)] for _ in range(3)]
        for (ref, q), hit in zip(sources, masks):

            def chosen(f):
                a, b, c = (ref[q, 16 * k + 8 * f : 16 * k + 8 * f + 8, :] for k in range(3))
                return jnp.where(near, a, jnp.where(middle, b, c))

            real, imag = chosen(0), chosen(1)
            fields = (real, imag, jnp.sqrt(real * real + imag * imag))
            for f in range(3):
                for m in range(4):
                    sums[f][m] += jnp.where(hit[m], fields[f], 0.0)
        for m in range(4):
            divisor = jnp.maximum(counts[m], 1.0)
            for f in range(3):
                value = sums[f][m] / divisor
                for s in range(8):
                    cols = slice(s * LANES, (s + 1) * LANES)
                    if f < 2:
                        ifg[pair, f, m : m + 1, cols] = value[s : s + 1]
                    else:
                        coh[pair, m : m + 1, cols] = value[s : s + 1]


def summing_weights():
    column = np.arange(5 * LANES)
    look = np.arange(LANES) % 32
    table = (column[:, None] // LOOK_C == look[None, :]).astype(np.float32)
    return jnp.asarray(table, jnp.bfloat16)


def passed_along(block, axis, distance):
    devices = range(lax.axis_size(axis))
    route = [(i - distance, i) for i in devices if i - distance in devices]
    return lax.ppermute(block, axis, route)


def moved_layers(block, step, layers=range(LAYERS)):
    route = [
        (RING * z + x, RING * (z + step) + x)
        for z in layers
        for x in range(RING)
        if z + step in range(LAYERS)
    ]
    return lax.ppermute(block, "date", route)


def in_ring(block):
    rings = [[RING * z + x for x in range(RING)] for z in range(LAYERS)]
    return lax.all_to_all(
        block, "date", split_axis=0, concat_axis=0, tiled=True, axis_index_groups=rings
    )


def looks_scratch(part, passes):
    edges, powers, fold = fold_rows(part, passes)
    f32 = jnp.float32
    return [
        pltpu.VMEM((2, edges * ROWS[part], LANES), f32),
        pltpu.VMEM((powers * ROWS[part], LANES), f32),
        pltpu.VMEM((fold, 5 * LANES), f32),
        pltpu.VMEM((edges * SPAN[part], LANES), f32),
    ]


def body(radar_image_cube, orbit_separations, epoch_couple_matrix, averaged_line_grid_lines):
    f32, bf16 = jnp.float32, jnp.bfloat16
    smem = pl.BlockSpec(memory_space=pltpu.SMEM)
    vmem = pl.BlockSpec(memory_space=pltpu.VMEM)
    hbm = pl.BlockSpec(memory_space=pltpu.HBM)

    def table(*shape, dtype=f32):
        return jax.ShapeDtypeStruct(shape, dtype)

    def call(kernel, outs, name, ins, scratch=(), limit=8, scalars=0, flops=0, moved=4_000_000, far=0):
        return pl.pallas_call(
            kernel,
            out_shape=outs,
            in_specs=[smem] * scalars + [vmem] * (len(ins) - scalars - far) + [hbm] * far,
            out_specs=[vmem] * len(outs),
            scratch_shapes=list(scratch),
            compiler_params=pltpu.CompilerParams(vmem_limit_bytes=limit << 20),
            cost_estimate=pl.CostEstimate(
                flops=flops, bytes_accessed=moved, transcendentals=0
            ),
            name=name,
        )(*ins)

    cube = radar_image_cube.reshape(2, 20, 160, LANES)
    cube = cube.transpose(1, 2, 0, 3).reshape(RING, LOOK_R * ALL_ROWS, LANES)
    separation = orbit_separations.reshape(1, 1)
    weights = summing_weights()
    sent, raw = call(
        first_pack,
        (table(RING, CHUNK[0], LANES, dtype=bf16), table(RING, CHUNK[1], LANES, dtype=bf16)),
        "first_pack",
        (cube, separation),
    )
    got = in_ring(sent)
    down = moved_layers(raw, -1)
    up = moved_layers(raw, 1, (LAYERS - 2,))
    both, splats = call(
        second_pack,
        (table(RING, 2 * CHUNK[1], LANES, dtype=bf16), table(24, LANES)),
        "second_pack",
        (averaged_line_grid_lines, epoch_couple_matrix, raw, down, up),
        scalars=2,
    )
    got_late = in_ring(both)
    strip = got[0:3]
    strip, again = lax.optimization_barrier((strip, got))
    onward = moved_layers(strip, -1)
    backward = moved_layers(again[1:4], 1, (LAYERS - 2,))
    inner, powers = call(
        inner_kernel,
        (table(12 * SPAN[0], LANES), table(4 * SPAN[0], LANES)),
        "inner_looks",
        (got, weights),
        looks_scratch(0, INNER),
        12,
        flops=10_000_000,
    )
    (turned,) = call(
        turn_kernel,
        (table(4 * SPAN[0], LANES),),
        "turned_looks",
        (got, powers, weights, backward),
        [pltpu.VMEM((3, CHUNK[0], LANES), bf16), pltpu.SemaphoreType.DMA]
        + looks_scratch(0, TURN_BACK),
        12,
        flops=10000000,
        moved=4000000,
        far=1,
    )
    (outer,) = call(
        outer_kernel,
        (table(12 * SPAN[0], LANES),),
        "outer_looks",
        (got, onward, powers, weights),
        looks_scratch(0, OUTER),
        12,
        flops=10_000_000,
    )
    (late,) = call(
        late_kernel,
        (table(24 * SPAN[1], LANES),),
        "late_looks",
        (got_late, weights),
        looks_scratch(1, LATE),
        12,
        flops=10_000_000,
    )
    (by_owner,) = call(
        gather_kernel,
        (table(RING, 56, LANES),),
        "by_owner",
        (splats, inner, outer, turned, late),
        limit=4,
    )
    own = in_ring(by_owner)
    below = passed_along(own, "band", 1)
    above = passed_along(own, "band", -1)
    return tuple(
        call(
            map_kernel,
            (table(2, 2, 4, 1024), table(2, 4, 1024)),
            "map_rows",
            (splats, below, own, above),
            limit=4,
        )
    )


def solution(mesh):
    placed = (P("date", None, "band", None), P("date"), P("date", None), P("band"))
    return jax.shard_map(
        body,
        mesh=mesh,
        in_specs=placed,
        out_specs=(P("date", None, "band", None), P("date", "band", None)),
        check_vma=False,
    )
```
